128 devices in a mesh: fsdp: 8 (over z, x_hi), tp: 16 (over x_lo, y, core).
Axes of the slice: x: 4 (x_hi: 2, x_lo: 2; x = x_hi * 2 + x_lo), y: 4, z: 4, core: 2. Of those that a mesh axis runs over, the one named last changes fastest.
Arguments:
- momentum: float32 [3584, 18432], P('fsdp', 'tp'), may hold values from -1500 to 1500
Outputs:
- update: float32 [3584, 18432], P('fsdp', 'tp')
The draws below stay inside these ranges and needn't reach their ends.
All inputs are finite; a program needn't handle non-finite values.
Results may differ from the reference program's by a relative error of at most 0.008.
Values may be sent and summed in bfloat16 or wider, within the bound.
No kernel may reach another device: no remote copies, remote signals or barrier semaphores. Data moves between devices by JAX's collectives and lax.ppermute only.
A program may use at most 64 MiB of HBM per device.

```python
import math
import jax
import jax.numpy as jnp
from jax import lax

M = 3584
N = 18432
ROUNDS = 2
N_TP = 16


def draw_momentum(key, part):
    key = jax.random.fold_in(key, 11)
    key_base, key_rows, key_cols, key_shared = jax.random.split(key, 4)
    row_pos = jnp.arange(M, dtype=jnp.float32) / M
    row_scale = 3.0 ** row_pos * 10.0 ** jax.random.uniform(key_rows, (M,), jnp.float32)
    col_scale = 10.0 ** jax.random.uniform(key_cols, (N,), jnp.float32)
    shared = jnp.clip(jax.random.normal(key_shared, (N,), jnp.float32), -5.0, 5.0)
    base = jnp.clip(jax.random.normal(key_base, (M, N), jnp.float32), -5.0, 5.0)
    base = 0.8 * base + 0.6 * shared[None, :]
    return (base * row_scale[:, None] * col_scale[None, :]).astype(jnp.float32)


def setup_inputs(seed: int = 0) -> dict:
    seeds = jax.random.split(jax.random.key(seed), 2)
    return {
        "momentum": draw_momentum(jax.random.fold_in(seeds[1], 71), 0),
    }


coef_linear = 3.4445
coef_cubic = -4.775
coef_quintic = 2.0315

def gram_of(scaled):
    width = N // N_TP

    def add_block(running, block_index):
        panel = lax.dynamic_slice_in_dim(scaled, (block_index * width).astype(jnp.int32), width, 1)
        term = lax.dot_general(panel, panel, (((1,), (1,)), ((), ())), preferred_element_type=jnp.float32)
        rounded = lax.optimization_barrier(term.astype(jnp.bfloat16))
        return (running + rounded.astype(jnp.float32), None)
    start = jnp.zeros((M, M), jnp.float32)
    result, unused = lax.scan(add_block, start, jnp.arange(N_TP, dtype=jnp.int32))
    return result

def reference(momentum):
    squares = jnp.sum(momentum * momentum)
    scaled = (momentum / (jnp.sqrt(squares) + 1e-07)).astype(jnp.bfloat16)
    updated = scaled.astype(jnp.float32)
    for turn_index in range(ROUNDS):
        gram_a = gram_of(scaled).astype(jnp.bfloat16)
        square = jnp.dot(gram_a, gram_a, preferred_element_type=jnp.float32)
        step_b = (coef_cubic * gram_a.astype(jnp.float32) + coef_quintic * square).astype(jnp.bfloat16)
        updated = coef_linear * scaled.astype(jnp.float32) + jnp.dot(step_b, scaled, preferred_element_type=jnp.float32)
        if turn_index + 1 < ROUNDS:
            scaled = updated.astype(jnp.bfloat16)
    return updated * math.sqrt(N)
```

```python
import functools
import math

import jax
import jax.numpy as jnp
from jax import lax
from jax.experimental import pallas as pl
from jax.experimental.pallas import tpu as pltpu
from jax.sharding import Mesh, PartitionSpec as P

coef_linear = 3.4445
coef_cubic = -4.775
coef_quintic = 2.0315

SIZES = (4, 2, 2, 4, 2)
BF = jnp.bfloat16
F32 = jnp.float32
ROWS = 448
SUB = 224
HALF = 112
COLS = 1152
VMEM = 60 * 1024 * 1024


def flat(pos):
    index = 0
    for value, size in zip(pos, SIZES):
        index = index * size + value
    return index


def positions():
    for z in range(4):
        for xh in range(2):
            for xl in range(2):
                for y in range(4):
                    for c in range(2):
                        yield (z, xh, xl, y, c)


def move(value, target):
    pairs = [(flat(pos), flat(target(*pos))) for pos in positions()]
    return lax.ppermute(value, ("z", "xh", "xl", "y", "c"), pairs)


def along_z(value, step):
    return move(value, lambda z, xh, xl, y, c: ((z - step) % 4, xh, xl, y, c))


def along_x(value, step):
    def target(z, xh, xl, y, c):
        x = (xh * 2 + xl - step) % 4
        return (z, x // 2, x % 2, y, c)

    return move(value, target)


def along_y(value, step):
    return move(value, lambda z, xh, xl, y, c: (z, xh, xl, (y - step) % 4, c))


def other_core(value):
    return move(value, lambda z, xh, xl, y, c: (z, xh, xl, y, 1 - c))


def trade_roles(value):
    return move(value, lambda z, xh, xl, y, c: (z, c, xl, y, xh))


def put(buffer, value, *index):
    zero = jnp.int32(0)
    tail = (zero,) * (buffer.ndim - len(index))
    lead = tuple(jnp.int32(i) for i in index)
    shape = (1,) * (buffer.ndim - value.ndim) + value.shape
    return lax.dynamic_update_slice(buffer, value.reshape(shape), lead + tail)


def take(buffer, axis, index):
    return lax.dynamic_index_in_dim(buffer, index, axis, keepdims=False)


def gram_kernel(order_ref, own_ref, *refs):
    parts, out_ref = refs[:-1], refs[-1]
    for i, part in enumerate(parts):
        out_ref[order_ref[i]] = lax.dot_general(
            part[...], own_ref[...], (((1,), (1,)), ((), ())), preferred_element_type=F32
        ).astype(BF)


def gram(order, own, parts):
    return pl.pallas_call(
        gram_kernel,
        out_shape=jax.ShapeDtypeStruct((8, ROWS, ROWS), BF),
        in_specs=[pl.BlockSpec(memory_space=pltpu.SMEM)]
        + [pl.BlockSpec(memory_space=pltpu.VMEM)] * (1 + len(parts)),
        out_specs=pl.BlockSpec(memory_space=pltpu.VMEM),
        compiler_params=pltpu.CompilerParams(vmem_limit_bytes=VMEM),
        cost_estimate=pl.CostEstimate(flops=2 * 8 * ROWS * ROWS * COLS, bytes_accessed=12 << 20, transcendentals=0),
        name="gram",
    )(order, own, *parts)


def mul_kernel(weights, order_ref, right_ref, *refs):
    out_ref = refs[-1]
    lefts, extras = refs[:8], refs[8:-1]
    total = jnp.zeros((SUB, ROWS), F32)
    for i in range(8):
        total += jnp.dot(lefts[i][...], right_ref[order_ref[i]], preferred_element_type=F32)
    total = total * weights[0]
    for weight, extra in zip(weights[1:], extras):
        total += weight * extra[...].astype(F32)
    out_ref[...] = total.astype(BF)


def mul(order, lefts, right, weights, extras):
    return pl.pallas_call(
        functools.partial(mul_kernel, weights),
        out_shape=jax.ShapeDtypeStruct((SUB, ROWS), BF),
        in_specs=[pl.BlockSpec(memory_space=pltpu.SMEM)]
        + [pl.BlockSpec(memory_space=pltpu.VMEM)] * (9 + len(extras)),
        out_specs=pl.BlockSpec(memory_space=pltpu.VMEM),
        compiler_params=pltpu.CompilerParams(vmem_limit_bytes=VMEM),
        cost_estimate=pl.CostEstimate(flops=2 * SUB * ROWS * 3584, bytes_accessed=6 << 20, transcendentals=0),
        name="mul",
    )(order, right, *lefts, *extras)


def apply_kernel(order_ref, scale_ref, mat_ref, *refs):
    parts, out_ref = refs[:-1], refs[-1]
    total = coef_linear * coef_linear * parts[0][...].astype(F32)
    for i, part in enumerate(parts):
        total += lax.dot_general(
            mat_ref[order_ref[i]], part[...], (((0,), (0,)), ((), ())), preferred_element_type=F32
        )
    out_ref[...] = total * scale_ref[0]


def apply(order, scale, mat, parts, width=384):
    return pl.pallas_call(
        apply_kernel,
        grid=(COLS // width,),
        out_shape=jax.ShapeDtypeStruct((ROWS, COLS), F32),
        in_specs=[
            pl.BlockSpec(memory_space=pltpu.SMEM),
            pl.BlockSpec(memory_space=pltpu.SMEM),
            pl.BlockSpec((8, ROWS, ROWS), lambda i: (0, 0, 0)),
        ]
        + [pl.BlockSpec((ROWS, width), lambda i: (0, i))] * 8,
        out_specs=pl.BlockSpec((ROWS, width), lambda i: (0, i)),
        compiler_params=pltpu.CompilerParams(vmem_limit_bytes=VMEM),
        cost_estimate=pl.CostEstimate(flops=2 * 8 * ROWS * ROWS * COLS, bytes_accessed=14 << 20, transcendentals=0),
        name="apply",
    )(order, scale, mat, *parts)


def gather_rows(value):
    pieces = [value] + [along_z(value, step) for step in (1, 3, 2)]
    steps = (0, 1, 3, 2)
    both = {}
    for step, piece in zip(steps, pieces):
        both[step] = (piece, other_core(piece))
    return [both[step][swap] for step in range(4) for swap in range(2)]


def gather_plane(value, x, y):
    first, second = value[:HALF], value[HALF:]
    lines_x = [first] + [along_x(first, s) for s in (1, 2, 3)]
    lines_y = [second] + [along_y(second, s) for s in (1, 2, 3)]
    stack_x = jnp.zeros((4, HALF, ROWS), BF)
    stack_y = jnp.zeros((4, HALF, ROWS), BF)
    for s in range(4):
        stack_x = put(stack_x, lines_x[s], (x + s) % 4)
        stack_y = put(stack_y, lines_y[s], (y + s) % 4)
    full_x = [stack_x] + [along_y(stack_x, s) for s in (1, 2, 3)]
    full_y = [stack_y] + [along_x(stack_y, s) for s in (1, 2, 3)]
    out = jnp.zeros((4, 4, 2, HALF, ROWS), BF)
    zero = jnp.int32(0)
    for s in range(4):
        out = lax.dynamic_update_slice(out, full_x[s].reshape(4, 1, 1, HALF, ROWS), (zero, (y + s) % 4, zero, zero, zero))
        out = lax.dynamic_update_slice(out, full_y[s].reshape(1, 4, 1, HALF, ROWS), ((x + s) % 4, zero, zero + 1, zero, zero))
    return out.reshape(8, ROWS, ROWS)


def scatter_plane(value, x, y):
    view = value.reshape(4, 4, 2, HALF, ROWS)
    first, second = view[:, :, 0], view[:, :, 1]
    sum_x = take(first, 0, x).astype(F32)
    sum_y = take(second, 1, y).astype(F32)
    for s in (1, 2, 3):
        sum_x += along_x(take(first, 0, (x - s) % 4), s).astype(F32)
        sum_y += along_y(take(second, 1, (y - s) % 4), s).astype(F32)
    sum_x, sum_y = sum_x.astype(BF), sum_y.astype(BF)
    one = take(sum_x, 0, y).astype(F32)
    two = take(sum_y, 0, x).astype(F32)
    for s in (1, 2, 3):
        one += along_y(take(sum_x, 0, (y - s) % 4), s).astype(F32)
        two += along_x(take(sum_y, 0, (x - s) % 4), s).astype(F32)
    return jnp.concatenate([one, two], 0)


def sum_all(value):
    value = value + other_core(value)
    value = value + along_z(value, 1) + along_z(value, 2) + along_z(value, 3)
    value = value + along_x(value, 1) + along_x(value, 2) + along_x(value, 3)
    return value + along_y(value, 1) + along_y(value, 2) + along_y(value, 3)


def body(momentum):
    z = lax.axis_index("z")
    x = lax.axis_index("xh") * 2 + lax.axis_index("xl")
    y = lax.axis_index("y")
    c = lax.axis_index("c")
    same = lax.axis_index("xh") == c
    order = jnp.stack(
        [((z + step) % 4) * 2 + (c if swap == 0 else 1 - c) for step in range(4) for swap in range(2)]
    ).astype(jnp.int32)

    own = trade_roles(momentum.astype(BF))
    squares = sum_all(jnp.sum(momentum * momentum).reshape(1, 1))
    scale = 1.0 / (jnp.sqrt(squares) + 1e-07)
    parts = gather_rows(own)
    share = scatter_plane(gram(order, own, parts), x, y)
    a = (share * scale * scale).astype(BF)

    a_left = gather_rows(a)
    a_right = gather_plane(a, x, y)
    b = mul(order, a_left, a_right, (coef_quintic, coef_cubic), (a,))
    b_left = gather_rows(b)
    b_right = gather_plane(b, x, y)
    v = mul(order, b_left, a_right, (1.0, coef_linear), (a,))
    a2 = mul(order, gather_rows(v), b_right, (1.0, coef_linear), (v,))
    a2_left = gather_rows(a2)
    a2_right = gather_plane(a2, x, y)
    h = mul(order, a2_left, b_right, (1.0, coef_linear), (a2,))
    d = mul(order, gather_rows(h), a2_right, (coef_quintic, coef_cubic, coef_linear), (h, b))
    d_right = gather_plane(d, x, y)
    update = apply(order, (scale * math.sqrt(18432)).reshape(1), d_right, parts)
    return jnp.where(same, update, trade_roles(update.astype(BF)).astype(F32))


def solution(mesh):
    names = ("z", "xh", "xl", "y", "c")
    split = Mesh(mesh.devices.reshape(SIZES), names)
    placed = P(("z", "xh"), ("xl", "y", "c"))
    return jax.shard_map(body, mesh=split, in_specs=(placed,), out_specs=placed, check_vma=False)
```

```python
import functools
import math

import jax
import jax.numpy as jnp
import numpy as np
from jax import lax
from jax.experimental import pallas as pl
from jax.experimental.pallas import tpu as pltpu
from jax.sharding import Mesh, PartitionSpec as P

coef_linear = 3.4445
coef_cubic = -4.775
coef_quintic = 2.0315

NAMES = ("z", "xh", "xl", "y", "c")
SIZES = (4, 2, 2, 4, 2)
PLANE = ("xh", "xl", "y")
BF = jnp.bfloat16
F32 = jnp.float32
ROWS = 448
SUB = 224
TAIL = 240
COLS = 1152
ALL = 3584
TILE = 128
WIDE = 512
VMEM = 60 * 1024 * 1024

def flat(pos):
    index = 0
    for value, size in zip(pos, SIZES):
        index = index * size + value
    return index


def move(value, target):
    every = [(z, a, b, y, c) for z in range(4) for a in range(2) for b in range(2) for y in range(4) for c in range(2)]
    return lax.ppermute(value, NAMES, [(flat(pos), flat(target(*pos))) for pos in every])


def swap_z(value, by):
    return move(value, lambda z, xh, xl, y, c: (z ^ by, xh, xl, y, c))


def other_core(value):
    return move(value, lambda z, xh, xl, y, c: (z, xh, xl, y, 1 - c))


def trade_roles(value):
    return move(value, lambda z, xh, xl, y, c: (z, c, xl, y, xh))


def struct(*shape, dtype=BF):
    return jax.ShapeDtypeStruct(shape, dtype)


def call(kernel, shapes, counts, name, flops, scratch=(), scalars_out=0):
    smem, vmem = counts
    n = len(shapes)
    return pl.pallas_call(
        kernel,
        out_shape=shapes,
        in_specs=[pl.BlockSpec(memory_space=pltpu.SMEM)] * smem + [pl.BlockSpec(memory_space=pltpu.VMEM)] * vmem,
        out_specs=[pl.BlockSpec(memory_space=pltpu.VMEM)] * (n - scalars_out)
        + [pl.BlockSpec(memory_space=pltpu.SMEM)] * scalars_out,
        scratch_shapes=list(scratch),
        compiler_params=pltpu.CompilerParams(vmem_limit_bytes=VMEM),
        cost_estimate=pl.CostEstimate(flops=flops, bytes_accessed=6 << 20, transcendentals=0),
        name=name,
    )


def split_value(value):
    lane = lax.broadcasted_iota(jnp.int32, (16, TILE), 1)
    whole = jnp.full((16, TILE), value, F32)
    high = whole.astype(BF).astype(F32)
    middle = (whole - high).astype(BF).astype(F32)
    low = whole - high - middle
    out = jnp.where(lane == 0, high, jnp.where(lane == 1, middle, jnp.where(lane == 2, low, 0.0)))
    return out.astype(BF)


def cast_kernel(in_ref, upper_ref, lower_ref):
    squares = jnp.zeros((8, COLS), F32)
    for i in range(0, ROWS, 32):
        block = in_ref[i : i + 32, :]
        if i < SUB:
            upper_ref[i : i + 32, :] = block.astype(BF)
        else:
            lower_ref[i - SUB : i - SUB + 32, :] = block.astype(BF)
        square = block * block
        squares += (square[:8] + square[8:16]) + (square[16:24] + square[24:])
    lower_ref[SUB:, :] = jnp.zeros((TAIL - SUB, COLS), BF)
    lower_ref[SUB:, :TILE] = split_value(jnp.sum(squares))


def cast(momentum):
    return call(cast_kernel, [struct(SUB, COLS), struct(TAIL, COLS)], (0, 1), "cast", 0)(momentum)


def pieces(refs):
    for ref in refs:
        step = ref.shape[0] // 2
        for i in range(2):
            yield ref[i * step : i * step + SUB, :]


def sum_of_squares(refs):
    total = jnp.zeros((), F32)
    for ref in refs:
        if ref.shape[0] == 2 * TAIL:
            for i in range(2):
                total += jnp.sum(ref[i * TAIL + SUB : (i + 1) * TAIL, :TILE].astype(F32)) * 0.0625
    return total


def turn(upper_ref, lower_ref, turned):
    turned[:, :SUB] = upper_ref[:SUB, :].T
    turned[:, SUB:] = lower_ref[:SUB, :].T


def gram_kernel(*refs):
    parts, out_ref, turned = refs[:-2], refs[-2], refs[-1]
    turn(parts[0], parts[1], turned)
    for i, piece in enumerate(pieces(parts)):
        out_ref[i] = jnp.dot(piece, turned[...], preferred_element_type=F32).astype(BF)


def gram(parts):
    flops = 2 * 2 * len(parts) * SUB * ROWS * COLS
    scratch = [pltpu.VMEM((COLS, ROWS), BF)]
    return call(gram_kernel, [struct(2 * len(parts), SUB, ROWS)], (0, len(parts)), "gram", flops, scratch)(*parts)[0]


def gram_more_kernel(count, order_ref, done_ref, *refs):
    parts, fresh, (out_ref, value_ref, turned) = refs[:count], refs[count : 2 * count], refs[2 * count :]
    turn(parts[0], parts[1], turned)
    for n in range(2 * count):
        out_ref[order_ref[n]] = done_ref[n]
    for n, piece in enumerate(pieces(fresh)):
        out_ref[order_ref[2 * count + n]] = jnp.dot(piece, turned[...], preferred_element_type=F32).astype(BF)
    value_ref[0] = sum_of_squares(parts) + sum_of_squares(fresh)


def gram_more(order, done, parts, fresh):
    count = len(parts)
    return call(
        functools.partial(gram_more_kernel, count),
        [struct(16, SUB, ROWS), struct(1, dtype=F32)],
        (1, 1 + 2 * count),
        "gram",
        2 * 2 * count * SUB * ROWS * COLS,
        [pltpu.VMEM((COLS, ROWS), BF)],
        scalars_out=1,
    )(order, done, *parts, *fresh)


def panel_kernel(order_ref, *refs):
    parts, out_ref = refs[:-1], refs[-1]
    for i, piece in enumerate(pieces(parts)):
        out_ref[order_ref[i]] = piece


def sum_kernel(value_ref, shares_ref, out_ref):
    total = shares_ref[0].astype(F32)
    for i in range(1, 16):
        total += shares_ref[i].astype(F32)
    out_ref[:, :ROWS] = total.astype(BF)
    out_ref[:, ROWS:] = jnp.zeros((SUB, WIDE - ROWS), BF)
    out_ref[:16, ROWS:] = split_value(value_ref[0])[:, : WIDE - ROWS]


def sum_shares(value, shares):
    return call(sum_kernel, [struct(SUB, WIDE)], (1, 1), "sum", 0)(value, shares)[0]


def fill_left(core_ref, mine_ref, other_ref, left):
    first = core_ref[0] == 0
    for i in range(4):
        mine, other = mine_ref[i, :, :ROWS], other_ref[i, :, :ROWS]
        left[:, i * 896 : i * 896 + ROWS] = jnp.where(first, mine, other)
        left[:, i * 896 + ROWS : (i + 1) * 896] = jnp.where(first, other, mine)


def first_kernel(core_ref, mine_ref, other_ref, right_ref, share_ref, out_ref, weight_ref, left):
    squares = jnp.zeros((), F32)
    for i in range(16):
        squares += jnp.sum(right_ref[i * SUB : i * SUB + 16, ROWS:].astype(F32)) * 0.0625
    scale = 1.0 / (jnp.sqrt(jnp.full((8, TILE), squares, F32)) + 1e-07)
    scale = jnp.max(scale)
    twice = scale * scale
    fill_left(core_ref, mine_ref, other_ref, left)
    total = jnp.dot(left[...], right_ref[:, :ROWS], preferred_element_type=F32)
    total = total * twice * (coef_quintic * twice) + (coef_cubic * twice) * share_ref[:, :ROWS].astype(F32)
    out_ref[...] = total.astype(BF)
    weight_ref[0] = twice
    weight_ref[1] = coef_linear * twice
    weight_ref[2] = scale * math.sqrt(18432)


def first_mul(core, lefts, right, share):
    return call(
        first_kernel,
        [struct(SUB, ROWS), struct(3, dtype=F32)],
        (1, 4),
        "first_mul",
        2 * SUB * ROWS * ALL,
        [pltpu.VMEM((SUB, ALL), BF)],
        scalars_out=1,
    )(core, *lefts, right, share)


def mul_kernel(weights, core_ref, weight_ref, mine_ref, other_ref, right_ref, *refs):
    extras, out_ref, left = refs[:-2], refs[-2], refs[-1]
    if weights is None:
        weights = [weight_ref[0], weight_ref[1]]
    fill_left(core_ref, mine_ref, other_ref, left)
    total = jnp.dot(left[...], right_ref[:, :ROWS], preferred_element_type=F32) * weights[0]
    for weight, extra in zip(weights[1:], extras):
        total += weight * extra[:, :ROWS].astype(F32)
    out_ref[...] = total.astype(BF)


def mul(core, weight, lefts, right, weights, extras):
    return call(
        functools.partial(mul_kernel, weights),
        [struct(SUB, ROWS)],
        (2, 3 + len(extras)),
        "mul",
        2 * SUB * ROWS * ALL,
        [pltpu.VMEM((SUB, ALL), BF)],
    )(core, weight, *lefts, right, *extras)[0]


def apply_kernel(weight_ref, upper_ref, lower_ref, panel_ref, right_ref, out_ref, send_ref, mat):
    for k in range(8):
        mat[:, k * ROWS : (k + 1) * ROWS] = right_ref[k * ROWS : (k + 1) * ROWS, :].T
    linear = coef_linear * coef_linear
    for i, own in ((0, upper_ref), (SUB, lower_ref)):
        total = jnp.dot(mat[i : i + SUB, :], panel_ref[...], preferred_element_type=F32)
        total = (total + linear * own[:SUB, :].astype(F32)) * weight_ref[2]
        out_ref[i : i + SUB, :] = total
        send_ref[i : i + SUB, :] = total.astype(BF)


def apply(weight, upper, lower, panel, right):
    return call(
        apply_kernel,
        [struct(ROWS, COLS, dtype=F32), struct(ROWS, COLS)],
        (1, 4),
        "apply",
        2 * ALL * ROWS * COLS,
        [pltpu.VMEM((ROWS, ALL), BF)],
    )(weight, upper, lower, panel, right)


def gather_rows(value):
    mine = lax.all_gather(value, "z")
    return [mine, other_core(mine)]


def gather_plane(value):
    return lax.all_gather(value, PLANE, axis=0, tiled=True)


def body(momentum):
    z, c = (lax.axis_index(name).astype(jnp.int32) for name in ("z", "c"))
    same = lax.axis_index("xh") == c
    core = c.reshape(1)

    upper, lower = (trade_roles(value) for value in cast(momentum))
    upper_1 = swap_z(upper, 1)
    lower_3 = swap_z(lower, 3)
    uppers = jnp.concatenate([upper, upper_1], 0)
    lowers = jnp.concatenate([lower, lower_3], 0)
    uppers_3 = swap_z(uppers, 3)
    lowers_1 = swap_z(lowers, 1)
    early = [uppers, lowers, other_core(uppers), other_core(lowers)]
    done = gram(early)
    uppers_3, lowers_1, done = lax.optimization_barrier((uppers_3, lowers_1, done))
    late = [uppers_3, lowers_1, other_core(uppers_3), other_core(lowers_1)]
    early_at = [(by, swap, half) for swap in (0, 1) for half in (0, 1) for by in ((0, 1) if half == 0 else (0, 3))]
    late_at = [(by, swap, half) for swap in (0, 1) for half in (0, 1) for by in ((3, 2) if half == 0 else (1, 2))]
    by, swap, half = (np.array(column, np.int32) for column in zip(*(early_at + late_at)))
    piece_x = z ^ by
    piece_y = (c ^ swap) * 2 + half
    order = piece_x * 4 + piece_y

    partial, value = gram_more(order, done, early, late)
    a = sum_shares(value, lax.all_to_all(partial, PLANE, 0, 0, tiled=True))
    panel = call(panel_kernel, [struct(16, SUB, COLS)], (1, 8), "panel", 0)(order, *early, *late)[0]
    panel = panel.reshape(ALL, COLS)

    a_right = gather_plane(a)
    b, weight = first_mul(core, gather_rows(a), a_right, a)

    b_right = gather_plane(b)
    v = mul(core, weight, gather_rows(b), a_right, None, (a,))
    a2 = mul(core, weight, gather_rows(v), b_right, (1.0, coef_linear), (v,))

    a2_right = gather_plane(a2)
    h = mul(core, weight, gather_rows(a2), b_right, (1.0, coef_linear), (a2,))
    d = mul(core, weight, gather_rows(h), a2_right, (coef_quintic, coef_cubic, coef_linear), (h, b))

    update, sent = apply(weight, upper, lower, panel, gather_plane(d))
    return jnp.where(same, update, trade_roles(sent).astype(F32))


def solution(mesh):
    split = Mesh(mesh.devices.reshape(SIZES), NAMES)
    placed = P(("z", "xh"), ("xl", "y", "c"))
    return jax.shard_map(body, mesh=split, in_specs=(placed,), out_specs=placed, check_vma=False)
```

```python
import functools
import math

import jax
import jax.numpy as jnp
import numpy as np
from jax import lax
from jax.experimental import pallas as pl
from jax.experimental.pallas import tpu as pltpu
from jax.sharding import Mesh, PartitionSpec as P

coef_linear = 3.4445
coef_cubic = -4.775
coef_quintic = 2.0315

NAMES = ("z", "xh", "xl", "y", "c")
SIZES = (4, 2, 2, 4, 2)
PLANE = ("xh", "xl", "y")
BF = jnp.bfloat16
F32 = jnp.float32
ROWS = 448
SUB = 224
TAIL = 240
COLS = 1152
ALL = 3584
TILE = 128
WIDE = 512
VMEM = 20 * 1024 * 1024
HALF = 256
REST = ROWS - HALF

def flat(pos):
    index = 0
    for value, size in zip(pos, SIZES):
        index = index * size + value
    return index


def move(value, target):
    every = [(z, a, b, y, c) for z in range(4) for a in range(2) for b in range(2) for y in range(4) for c in range(2)]
    return lax.ppermute(value, NAMES, [(flat(pos), flat(target(*pos))) for pos in every])


def swap_z(value, by):
    return move(value, lambda z, xh, xl, y, c: (z ^ by, xh, xl, y, c))


def along_x(value, step):
    def target(z, xh, xl, y, c):
        x = (xh * 2 + xl - step) % 4
        return (z, x // 2, x % 2, y, c)

    return move(value, target)


def along_y(value, step):
    return move(value, lambda z, xh, xl, y, c: (z, xh, xl, (y - step) % 4, c))


def swap_x(value, by):
    return move(value, lambda z, xh, xl, y, c: (z, xh ^ (by >> 1), xl ^ (by & 1), y, c))


def swap_y(value, by):
    return move(value, lambda z, xh, xl, y, c: (z, xh, xl, y ^ by, c))


def other_core(value):
    return move(value, lambda z, xh, xl, y, c: (z, xh, xl, y, 1 - c))


def trade_roles(value):
    return move(value, lambda z, xh, xl, y, c: (z, c, xl, y, xh))


def struct(*shape, dtype=BF):
    return jax.ShapeDtypeStruct(shape, dtype)


def call(kernel, shapes, counts, name, flops, scratch=(), scalars_out=0):
    smem, vmem = counts
    n = len(shapes)
    return pl.pallas_call(
        kernel,
        out_shape=shapes,
        in_specs=[pl.BlockSpec(memory_space=pltpu.SMEM)] * smem + [pl.BlockSpec(memory_space=pltpu.VMEM)] * vmem,
        out_specs=[pl.BlockSpec(memory_space=pltpu.VMEM)] * (n - scalars_out)
        + [pl.BlockSpec(memory_space=pltpu.SMEM)] * scalars_out,
        scratch_shapes=list(scratch),
        compiler_params=pltpu.CompilerParams(vmem_limit_bytes=VMEM),
        cost_estimate=pl.CostEstimate(flops=flops, bytes_accessed=6 << 20, transcendentals=0),
        name=name,
    )


def split_value(value):
    lane = lax.broadcasted_iota(jnp.int32, (16, TILE), 1)
    whole = jnp.full((16, TILE), value, F32)
    high = whole.astype(BF).astype(F32)
    middle = (whole - high).astype(BF).astype(F32)
    low = whole - high - middle
    out = jnp.where(lane == 0, high, jnp.where(lane == 1, middle, jnp.where(lane == 2, low, 0.0)))
    return out.astype(BF)


def cast_kernel(in_ref, upper_ref, lower_ref):
    squares = jnp.zeros((8, COLS), F32)
    for i in range(0, ROWS, 32):
        block = in_ref[i : i + 32, :]
        if i < SUB:
            upper_ref[i : i + 32, :] = block.astype(BF)
        else:
            lower_ref[i - SUB : i - SUB + 32, :] = block.astype(BF)
        square = block * block
        squares += (square[:8] + square[8:16]) + (square[16:24] + square[24:])
    lower_ref[SUB:, :] = jnp.zeros((TAIL - SUB, COLS), BF)
    lower_ref[SUB:, :TILE] = split_value(jnp.sum(squares))


def cast(momentum):
    return call(cast_kernel, [struct(SUB, COLS), struct(TAIL, COLS)], (0, 1), "cast", 0)(momentum)


def pieces(refs):
    for ref in refs:
        step = ref.shape[0] // 2
        for i in range(2):
            yield ref[i * step : i * step + SUB, :]


def sum_of_squares(refs):
    total = jnp.zeros((), F32)
    for ref in refs:
        if ref.shape[0] == 2 * TAIL:
            for i in range(2):
                total += jnp.sum(ref[i * TAIL + SUB : (i + 1) * TAIL, :TILE].astype(F32)) * 0.0625
    return total


def turn(upper_ref, lower_ref, turned):
    turned[:, :SUB] = upper_ref[:SUB, :].T
    turned[:, SUB:] = lower_ref[:SUB, :].T


def gram_kernel(*refs):
    parts, out_ref, turned = refs[:-2], refs[-2], refs[-1]
    turn(parts[0], parts[1], turned)
    for i, piece in enumerate(pieces(parts)):
        out_ref[i] = jnp.dot(piece, turned[...], preferred_element_type=F32).astype(BF)


def gram(parts):
    flops = 2 * 2 * len(parts) * SUB * ROWS * COLS
    scratch = [pltpu.VMEM((COLS, ROWS), BF)]
    return call(gram_kernel, [struct(2 * len(parts), SUB, ROWS)], (0, len(parts)), "gram", flops, scratch)(*parts)[0]


def gram_more_kernel(count, index_ref, done_ref, *refs):
    parts, fresh, outs = refs[:count], refs[count : 2 * count], refs[2 * count : 2 * count + 8]
    value_ref, turned, full = refs[2 * count + 8], refs[2 * count + 9], refs[2 * count + 10 :]
    turn(parts[0], parts[1], turned)

    def store(n, block):
        for q in range(4):
            end = min(TILE, ROWS - q * TILE)
            full[q][index_ref[q * 16 + n], :, :end] = block[:, q * TILE : q * TILE + end]

    for n in range(2 * count):
        store(n, done_ref[n])
    for n, piece in enumerate(pieces(fresh)):
        store(2 * count + n, jnp.dot(piece, turned[...], preferred_element_type=F32).astype(BF))
    for q in range(4):
        end = min(TILE, ROWS - q * TILE)
        for half in range(2):
            outs[2 * q + half][:, :, :end] = full[q][half * 8 : half * 8 + 8, :, :end]
            if end < TILE:
                outs[2 * q + half][:, :, end:] = jnp.zeros((8, SUB, TILE - end), BF)
    value_ref[0] = sum_of_squares(parts) + sum_of_squares(fresh)


def gram_more(index, done, parts, fresh):
    count = len(parts)
    return call(
        functools.partial(gram_more_kernel, count),
        [struct(8, SUB, TILE)] * 8 + [struct(1, dtype=F32)],
        (1, 1 + 2 * count),
        "gram",
        2 * 2 * count * SUB * ROWS * COLS,
        [pltpu.VMEM((COLS, ROWS), BF)] + [pltpu.VMEM((16, SUB, TILE), BF)] * 4,
        scalars_out=1,
    )(index, done, *parts, *fresh)


def panel_kernel(order_ref, *refs):
    parts, out_ref = refs[:-1], refs[-1]
    for i, piece in enumerate(pieces(parts)):
        out_ref[order_ref[i]] = piece


def halve_kernel(*refs):
    keep, got, outs = refs[:4], refs[4:8], refs[8:]
    for q in range(4):
        for i in range(8):
            total = keep[q][i].astype(F32) + got[q][i].astype(F32)
            outs[2 * q + i // 4][i % 4] = total.astype(BF)


def unstack_kernel(*refs):
    keep, got, outs = refs[:4], refs[4:8], refs[8:]
    for q in range(4):
        at = (q % 2) * TILE
        for i in range(4):
            total = keep[q][i].astype(F32) + got[q][i].astype(F32)
            outs[(q // 2) * 4 + i][:, at : at + TILE] = total.astype(BF)


def sum_kernel(value_ref, *refs):
    wides, rests, (out_ref, wide_ref, rest_ref) = refs[:4], refs[4:8], refs[8:]
    for refs, sum_ref in ((wides, wide_ref), (rests, rest_ref)):
        total = refs[0][...].astype(F32)
        for ref in refs[1:]:
            total += ref[...].astype(F32)
        sum_ref[...] = total.astype(BF)
    rest_ref[:16, REST:] = split_value(value_ref[0])[:, : HALF - REST]
    out_ref[:, :HALF] = wide_ref[...]
    out_ref[:, HALF:] = rest_ref[...]


def scatter_plane(split, value):
    keep, send = split[0::2], split[1::2]
    got = [swap_y(send[0], 3), swap_y(send[1], 1), swap_x(send[2], 3), swap_x(send[3], 1)]
    split = call(halve_kernel, [struct(4, SUB, TILE)] * 8, (0, 8), "halve", 0)(*keep, *got)
    keep, send = split[0::2], split[1::2]
    got = [swap_y(send[0], 1), swap_y(send[1], 3), swap_x(send[2], 1), swap_x(send[3], 3)]
    halves = call(unstack_kernel, [struct(SUB, HALF)] * 8, (0, 8), "unstack", 0)(*keep, *got)
    wides = [halves[0]] + [along_x(halves[s], -s) for s in (1, 2, 3)]
    rests = [halves[4]] + [along_y(halves[4 + s], -s) for s in (1, 2, 3)]
    shapes = [struct(SUB, WIDE), struct(SUB, HALF), struct(SUB, HALF)]
    return call(sum_kernel, shapes, (1, 8), "sum", 0)(value, *wides, *rests)


def stack_kernel(*refs):
    for n, outs in ((0, refs[8:10]), (4, refs[10:12])):
        for i in range(4):
            outs[0][i] = refs[n + i][:, :TILE]
            outs[1][i] = refs[n + i][:, TILE:]


def join_kernel(*refs):
    mine, got, outs = refs[:4], refs[4:8], refs[8:]
    for q in range(4):
        outs[q][:4] = mine[q][...]
        outs[q][4:] = got[q][...]


def gather_parts(wide, rest):
    wides = [wide] + [along_x(wide, s) for s in (1, 2, 3)]
    rests = [rest] + [along_y(rest, s) for s in (1, 2, 3)]
    parts = call(stack_kernel, [struct(4, SUB, TILE)] * 4, (0, 8), "stack", 0)(*wides, *rests)
    got = [swap_y(parts[0], 1), swap_y(parts[1], 3), swap_x(parts[2], 1), swap_x(parts[3], 3)]
    parts = call(join_kernel, [struct(8, SUB, TILE)] * 4, (0, 8), "join", 0)(*parts, *got)
    got = [swap_y(parts[0], 3), swap_y(parts[1], 1), swap_x(parts[2], 3), swap_x(parts[3], 1)]
    return [*parts, *got]


def place(pos_ref, refs, right):
    x, y = pos_ref[0], pos_ref[1]
    for q in range(4):
        end = min(TILE, right.shape[1] - q * TILE)
        first, second = ((1, 3), (3, 1))[q % 2]
        for i in range(16):
            by = (0, first, second, first ^ second)[i // 4]
            if q < 2:
                share = lax.rem(x + i % 4, 4) * 4 + (y ^ by)
            else:
                share = (x ^ by) * 4 + lax.rem(y + i % 4, 4)
            rows = pl.ds(pl.multiple_of(share * SUB, SUB), SUB)
            right[rows, q * TILE : q * TILE + end] = refs[q + (i // 8) * 4][i % 8, :, :end]


def product(core_ref, mine_ref, other_ref, right, left):
    first = core_ref[0] == 0
    for i in range(4):
        mine, other = mine_ref[i, :, :ROWS], other_ref[i, :, :ROWS]
        left[:, i * 896 : i * 896 + ROWS] = jnp.where(first, mine, other)
        left[:, i * 896 + ROWS : (i + 1) * 896] = jnp.where(first, other, mine)
    return jnp.dot(left[...], right[:, :ROWS], preferred_element_type=F32)


def first_kernel(core_ref, pos_ref, *refs):
    lefts, share_ref, refs = refs[:4], refs[4], refs[5:]
    parts, (out_ref, right_ref, weight_ref, left) = refs[:8], refs[8:]
    place(pos_ref, parts, right_ref)
    squares = jnp.zeros((), F32)
    for i in range(16):
        squares += jnp.sum(right_ref[i * SUB : i * SUB + 16, ROWS:].astype(F32)) * 0.0625
    scale = 1.0 / (jnp.sqrt(jnp.full((8, TILE), squares, F32)) + 1e-07)
    scale = jnp.max(scale)
    twice = scale * scale
    first = core_ref[0] == 0
    for i, by in enumerate((0, 1, 3, 2)):
        rows = slice(i % 2 * SUB, (i % 2 + 1) * SUB)
        mine, other = lefts[i // 2][rows, :ROWS], lefts[2 + i // 2][rows, :ROWS]
        line = jnp.concatenate([jnp.where(first, mine, other), jnp.where(first, other, mine)], 1)
        left[:, pl.ds(pl.multiple_of((pos_ref[2] ^ by) * 896, TILE), 896)] = line
    total = jnp.dot(left[...], right_ref[:, :ROWS], preferred_element_type=F32)
    total = total * twice * (coef_quintic * twice) + (coef_cubic * twice) * share_ref[:, :ROWS].astype(F32)
    out_ref[...] = total.astype(BF)
    weight_ref[0] = twice
    weight_ref[1] = coef_linear * twice
    weight_ref[2] = scale * math.sqrt(18432)


def first_mul(core, pos, lefts, share, parts):
    return call(
        first_kernel,
        [struct(SUB, ROWS), struct(ALL, WIDE), struct(3, dtype=F32)],
        (2, 13),
        "first_mul",
        2 * SUB * ROWS * ALL,
        [pltpu.VMEM((SUB, ALL), BF)],
        scalars_out=1,
    )(core, pos, *lefts, share, *parts)


def mul_kernel(weights, count, core_ref, weight_ref, mine_ref, other_ref, right_ref, *refs):
    extras, outs, left = refs[:count], refs[count:-1], refs[-1]
    if weights is None:
        weights = [weight_ref[0], weight_ref[1]]
    total = product(core_ref, mine_ref, other_ref, right_ref, left) * weights[0]
    for weight, extra in zip(weights[1:], extras):
        total += weight * extra[:, :ROWS].astype(F32)
    total = total.astype(BF)
    if len(outs) == 1:
        outs[0][...] = total
    else:
        outs[0][...] = total[:, :HALF]
        outs[1][:, :REST] = total[:, HALF:]
        outs[1][:, REST:] = jnp.zeros((SUB, HALF - REST), BF)


def mul(core, weight, lefts, right, weights, extras, halves=False):
    return call(
        functools.partial(mul_kernel, weights, len(extras)),
        [struct(SUB, HALF)] * 2 if halves else [struct(SUB, ROWS)],
        (2, 3 + len(extras)),
        "mul",
        2 * SUB * ROWS * ALL,
        [pltpu.VMEM((SUB, ALL), BF)],
    )(core, weight, *lefts, right, *extras)


def apply_kernel(weight_ref, pos_ref, upper_ref, lower_ref, panel_ref, *refs):
    parts, (out_ref, send_ref, right, mat) = refs[:8], refs[8:]
    place(pos_ref, parts, right)
    for k in range(8):
        mat[:, k * ROWS : (k + 1) * ROWS] = right[k * ROWS : (k + 1) * ROWS, :].T
    linear = coef_linear * coef_linear
    for i, own in ((0, upper_ref), (SUB, lower_ref)):
        total = jnp.dot(mat[i : i + SUB, :], panel_ref[...], preferred_element_type=F32)
        total = (total + linear * own[:SUB, :].astype(F32)) * weight_ref[2]
        out_ref[i : i + SUB, :] = total
        send_ref[i : i + SUB, :] = total.astype(BF)


def apply(weight, pos, upper, lower, panel, parts):
    return call(
        apply_kernel,
        [struct(ROWS, COLS, dtype=F32), struct(ROWS, COLS)],
        (2, 11),
        "apply",
        2 * ALL * ROWS * COLS,
        [pltpu.VMEM((ALL, ROWS), BF), pltpu.VMEM((ROWS, ALL), BF)],
    )(weight, pos, upper, lower, panel, *parts)


def gather_rows(value):
    mine = lax.all_gather(value, "z")
    return [mine, other_core(mine)]


def gather_plane(value):
    return lax.all_gather(value, PLANE, axis=0, tiled=True)


def body(momentum):
    z, c = (lax.axis_index(name).astype(jnp.int32) for name in ("z", "c"))
    same = lax.axis_index("xh") == c
    core = c.reshape(1)
    x = (lax.axis_index("xh") * 2 + lax.axis_index("xl")).astype(jnp.int32)
    y = lax.axis_index("y").astype(jnp.int32)
    pos = jnp.stack([x, y, z])

    upper, lower = (trade_roles(value) for value in cast(momentum))
    upper_1 = swap_z(upper, 1)
    lower_3 = swap_z(lower, 3)
    uppers = jnp.concatenate([upper, upper_1], 0)
    lowers = jnp.concatenate([lower, lower_3], 0)
    uppers_3 = swap_z(uppers, 3)
    lowers_1 = swap_z(lowers, 1)
    early = [uppers, lowers, other_core(uppers), other_core(lowers)]
    done = gram(early)
    uppers_3, lowers_1, done = lax.optimization_barrier((uppers_3, lowers_1, done))
    late = [uppers_3, lowers_1, other_core(uppers_3), other_core(lowers_1)]
    early_at = [(by, swap, half) for swap in (0, 1) for half in (0, 1) for by in ((0, 1) if half == 0 else (0, 3))]
    late_at = [(by, swap, half) for swap in (0, 1) for half in (0, 1) for by in ((3, 2) if half == 0 else (1, 2))]
    by, swap, half = (np.array(column, np.int32) for column in zip(*(early_at + late_at)))
    piece_x = z ^ by
    piece_y = (c ^ swap) * 2 + half
    order = piece_x * 4 + piece_y

    gray_x, gray_y = ((e ^ (e >> 1)) * 4 for e in (piece_x ^ x, piece_y ^ y))
    flip_x, flip_y = (((g & 4) * 2 + (g >> 1 & 4)) for g in (gray_x, gray_y))
    far_x, far_y = (piece_x - x) & 3, (piece_y - y) & 3
    index = jnp.concatenate([gray_y + far_x, flip_y + far_x, gray_x + far_y, flip_x + far_y])
    *split, value = gram_more(index, done, early, late)
    a, wide, rest = scatter_plane(split, value)
    near = jnp.concatenate([a, swap_z(a, 1)], 0)
    far = swap_z(near, 3)
    lefts = [near, far, other_core(near), other_core(far)]
    b, a_right, weight = first_mul(core, pos, lefts, a, gather_parts(wide, rest))

    b_right = gather_plane(b)
    (v,) = mul(core, weight, gather_rows(b), a_right, None, (a,))
    (a2,) = mul(core, weight, gather_rows(v), b_right, (1.0, coef_linear), (v,))

    a2_right = gather_plane(a2)
    (h,) = mul(core, weight, gather_rows(a2), b_right, (1.0, coef_linear), (a2,))
    weights = (coef_quintic, coef_cubic, coef_linear)
    wide, rest = mul(core, weight, gather_rows(h), a2_right, weights, (h, b), True)
    wide, rest, order = lax.optimization_barrier((wide, rest, order))
    panel = call(panel_kernel, [struct(16, SUB, COLS)], (1, 8), "panel", 0)(order, *early, *late)[0]
    panel = panel.reshape(ALL, COLS)

    update, sent = apply(weight, pos, upper, lower, panel, gather_parts(wide, rest))
    return jnp.where(same, update, trade_roles(sent).astype(F32))


def solution(mesh):
    split = Mesh(mesh.devices.reshape(SIZES), NAMES)
    placed = P(("z", "xh"), ("xl", "y", "c"))
    return jax.shard_map(body, mesh=split, in_specs=(placed,), out_specs=placed, check_vma=False)
```

```python
import functools
import math

import jax
import jax.numpy as jnp
import numpy as np
from jax import lax
from jax.experimental import pallas as pl
from jax.experimental.pallas import tpu as pltpu
from jax.sharding import Mesh, PartitionSpec as P

coef_linear = 3.4445
coef_cubic = -4.775
coef_quintic = 2.0315

NAMES = ("z", "xh", "xl", "y", "c")
SIZES = (4, 2, 2, 4, 2)
PLANE = ("xh", "xl", "y")
BF = jnp.bfloat16
F32 = jnp.float32
ROWS = 448
SUB = 224
TAIL = 240
COLS = 1152
ALL = 3584
TILE = 128
WIDE = 512
VMEM = 20 * 1024 * 1024
MOST = 60 * 1024 * 1024
HALF = 256
REST = ROWS - HALF

def flat(pos):
    index = 0
    for value, size in zip(pos, SIZES):
        index = index * size + value
    return index


def move(value, target):
    every = [(z, a, b, y, c) for z in range(4) for a in range(2) for b in range(2) for y in range(4) for c in range(2)]
    return lax.ppermute(value, NAMES, [(flat(pos), flat(target(*pos))) for pos in every])


def swap_z(value, by):
    return move(value, lambda z, xh, xl, y, c: (z ^ by, xh, xl, y, c))


def along_x(value, step):
    def target(z, xh, xl, y, c):
        x = (xh * 2 + xl - step) % 4
        return (z, x // 2, x % 2, y, c)

    return move(value, target)


def along_y(value, step):
    return move(value, lambda z, xh, xl, y, c: (z, xh, xl, (y - step) % 4, c))


def swap_x(value, by):
    return move(value, lambda z, xh, xl, y, c: (z, xh ^ (by >> 1), xl ^ (by & 1), y, c))


def swap_y(value, by):
    return move(value, lambda z, xh, xl, y, c: (z, xh, xl, y ^ by, c))


def other_core(value):
    return move(value, lambda z, xh, xl, y, c: (z, xh, xl, y, 1 - c))


def trade_roles(value):
    return move(value, lambda z, xh, xl, y, c: (z, c, xl, y, xh))


def struct(*shape, dtype=BF):
    return jax.ShapeDtypeStruct(shape, dtype)


def call(kernel, shapes, counts, name, flops, scratch=(), scalars_out=0, limit=VMEM):
    smem, vmem = counts
    n = len(shapes)
    return pl.pallas_call(
        kernel,
        out_shape=shapes,
        in_specs=[pl.BlockSpec(memory_space=pltpu.SMEM)] * smem + [pl.BlockSpec(memory_space=pltpu.VMEM)] * vmem,
        out_specs=[pl.BlockSpec(memory_space=pltpu.VMEM)] * (n - scalars_out)
        + [pl.BlockSpec(memory_space=pltpu.SMEM)] * scalars_out,
        scratch_shapes=list(scratch),
        compiler_params=pltpu.CompilerParams(vmem_limit_bytes=limit),
        cost_estimate=pl.CostEstimate(flops=flops, bytes_accessed=6 << 20, transcendentals=0),
        name=name,
    )


def split_value(value):
    lane = lax.broadcasted_iota(jnp.int32, (16, TILE), 1)
    whole = jnp.full((16, TILE), value, F32)
    high = whole.astype(BF).astype(F32)
    middle = (whole - high).astype(BF).astype(F32)
    low = whole - high - middle
    out = jnp.where(lane == 0, high, jnp.where(lane == 1, middle, jnp.where(lane == 2, low, 0.0)))
    return out.astype(BF)


def cast_kernel(in_ref, upper_ref, lower_ref):
    squares = jnp.zeros((8, COLS), F32)
    for i in range(0, ROWS, 32):
        block = in_ref[i : i + 32, :]
        if i < SUB:
            upper_ref[i : i + 32, :] = block.astype(BF)
        else:
            lower_ref[i - SUB : i - SUB + 32, :] = block.astype(BF)
        square = block * block
        squares += (square[:8] + square[8:16]) + (square[16:24] + square[24:])
    lower_ref[SUB:, :] = jnp.zeros((TAIL - SUB, COLS), BF)
    lower_ref[SUB:, :TILE] = split_value(jnp.sum(squares))


def cast(momentum):
    return call(cast_kernel, [struct(SUB, COLS), struct(TAIL, COLS)], (0, 1), "cast", 0)(momentum)


def pieces(refs):
    for ref in refs:
        step = ref.shape[0] // 2
        for i in range(2):
            yield ref[i * step : i * step + SUB, :]


def sum_of_squares(refs):
    total = jnp.zeros((), F32)
    for ref in refs:
        if ref.shape[0] == 2 * TAIL:
            for i in range(2):
                total += jnp.sum(ref[i * TAIL + SUB : (i + 1) * TAIL, :TILE].astype(F32)) * 0.0625
    return total


def turn(upper_ref, lower_ref, turned):
    turned[:, :SUB] = upper_ref[:SUB, :].T
    turned[:, SUB:] = lower_ref[:SUB, :].T


def gram_kernel(upper_ref, lower_ref, *refs):
    parts, out_ref, turned = refs[:-2], refs[-2], refs[-1]
    turn(upper_ref, lower_ref, turned)
    for i, piece in enumerate(pieces(parts or (upper_ref, lower_ref))):
        out_ref[i] = jnp.dot(piece, turned[...], preferred_element_type=F32).astype(BF)


def gram(*parts):
    scratch = [pltpu.VMEM((COLS, ROWS), BF)]
    flops = 2 * 4 * SUB * ROWS * COLS
    return call(gram_kernel, [struct(4, SUB, ROWS)], (0, len(parts)), "gram", flops, scratch)(*parts)[0]


def gram_more_kernel(count, index_ref, done_ref, more_ref, *refs):
    parts, fresh, outs = refs[:count], refs[count : 2 * count], refs[2 * count : 2 * count + 8]
    value_ref, turned, full = refs[2 * count + 8], refs[2 * count + 9], refs[2 * count + 10 :]
    turn(parts[0], parts[1], turned)

    def store(n, block):
        for q in range(4):
            end = min(TILE, ROWS - q * TILE)
            full[q][index_ref[q * 16 + n], :, :end] = block[:, q * TILE : q * TILE + end]

    for n in range(4):
        store(n, done_ref[n])
        store(4 + n, more_ref[n])
    for n, piece in enumerate(pieces(fresh)):
        store(2 * count + n, jnp.dot(piece, turned[...], preferred_element_type=F32).astype(BF))
    for q in range(4):
        end = min(TILE, ROWS - q * TILE)
        for half in range(2):
            outs[2 * q + half][:, :, :end] = full[q][half * 8 : half * 8 + 8, :, :end]
            if end < TILE:
                outs[2 * q + half][:, :, end:] = jnp.zeros((8, SUB, TILE - end), BF)
    value_ref[0] = sum_of_squares(parts) + sum_of_squares(fresh)


def gram_more(index, done, more, parts, fresh):
    count = len(parts)
    return call(
        functools.partial(gram_more_kernel, count),
        [struct(8, SUB, TILE)] * 8 + [struct(1, dtype=F32)],
        (1, 2 + 2 * count),
        "gram",
        2 * 2 * count * SUB * ROWS * COLS,
        [pltpu.VMEM((COLS, ROWS), BF)] + [pltpu.VMEM((16, SUB, TILE), BF)] * 4,
        scalars_out=1,
    )(index, done, more, *parts, *fresh)


def panel_kernel(order_ref, *refs):
    parts, out_ref = refs[:-1], refs[-1]
    for i, piece in enumerate(pieces(parts)):
        out_ref[order_ref[i]] = piece


def halve_kernel(*refs):
    keep, got, outs = refs[:4], refs[4:8], refs[8:]
    for q in range(4):
        for i in range(8):
            total = keep[q][i].astype(F32) + got[q][i].astype(F32)
            outs[2 * q + i // 4][i % 4] = total.astype(BF)


def unstack_kernel(*refs):
    keep, got, outs = refs[:4], refs[4:8], refs[8:]
    for q in range(4):
        at = (q % 2) * TILE
        for i in range(4):
            total = keep[q][i].astype(F32) + got[q][i].astype(F32)
            outs[(q // 2) * 4 + i][:, at : at + TILE] = total.astype(BF)


def sum_kernel(value_ref, *refs):
    wides, rests, (out_ref, wide_ref, rest_ref) = refs[:4], refs[4:8], refs[8:]
    for refs, sum_ref in ((wides, wide_ref), (rests, rest_ref)):
        total = refs[0][...].astype(F32)
        for ref in refs[1:]:
            total += ref[...].astype(F32)
        sum_ref[...] = total.astype(BF)
    rest_ref[:16, REST:] = split_value(value_ref[0])[:, : HALF - REST]
    out_ref[:, :HALF] = wide_ref[...]
    out_ref[:, HALF:] = rest_ref[...]


def scatter_plane(split, value):
    keep, send = split[0::2], split[1::2]
    got = [swap_y(send[0], 3), swap_y(send[1], 1), swap_x(send[2], 3), swap_x(send[3], 1)]
    split = call(halve_kernel, [struct(4, SUB, TILE)] * 8, (0, 8), "halve", 0)(*keep, *got)
    keep, send = split[0::2], split[1::2]
    got = [swap_y(send[0], 1), swap_y(send[1], 3), swap_x(send[2], 1), swap_x(send[3], 3)]
    halves = call(unstack_kernel, [struct(SUB, HALF)] * 8, (0, 8), "unstack", 0)(*keep, *got)
    wides = [halves[0]] + [along_x(halves[s], -s) for s in (1, 2, 3)]
    rests = [halves[4]] + [along_y(halves[4 + s], -s) for s in (1, 2, 3)]
    shapes = [struct(SUB, WIDE), struct(SUB, HALF), struct(SUB, HALF)]
    return call(sum_kernel, shapes, (1, 8), "sum", 0)(value, *wides, *rests)


def stack_kernel(*refs):
    for n, outs in ((0, refs[8:10]), (4, refs[10:12])):
        for i in range(4):
            outs[0][i] = refs[n + i][:, :TILE]
            outs[1][i] = refs[n + i][:, TILE:]


def join_kernel(*refs):
    mine, got, outs = refs[:4], refs[4:8], refs[8:]
    for q in range(4):
        outs[q][:4] = mine[q][...]
        outs[q][4:] = got[q][...]


def gather_parts(wide, rest):
    wides = [wide] + [along_x(wide, s) for s in (1, 2, 3)]
    rests = [rest] + [along_y(rest, s) for s in (1, 2, 3)]
    parts = call(stack_kernel, [struct(4, SUB, TILE)] * 4, (0, 8), "stack", 0)(*wides, *rests)
    got = [swap_y(parts[0], 1), swap_y(parts[1], 3), swap_x(parts[2], 1), swap_x(parts[3], 3)]
    parts = call(join_kernel, [struct(8, SUB, TILE)] * 4, (0, 8), "join", 0)(*parts, *got)
    got = [swap_y(parts[0], 3), swap_y(parts[1], 1), swap_x(parts[2], 3), swap_x(parts[3], 1)]
    return [*parts, *got]


def place(pos_ref, refs, right):
    x, y = pos_ref[0], pos_ref[1]
    for q in range(4):
        end = min(TILE, right.shape[1] - q * TILE)
        first, second = ((1, 3), (3, 1))[q % 2]
        for i in range(16):
            by = (0, first, second, first ^ second)[i // 4]
            if q < 2:
                share = lax.rem(x + i % 4, 4) * 4 + (y ^ by)
            else:
                share = (x ^ by) * 4 + lax.rem(y + i % 4, 4)
            rows = pl.ds(pl.multiple_of(share * SUB, SUB), SUB)
            right[rows, q * TILE : q * TILE + end] = refs[q + (i // 8) * 4][i % 8, :, :end]


def product(core_ref, mine_ref, other_ref, right, left):
    first = core_ref[0] == 0
    for i in range(4):
        mine, other = mine_ref[i, :, :ROWS], other_ref[i, :, :ROWS]
        left[:, i * 896 : i * 896 + ROWS] = jnp.where(first, mine, other)
        left[:, i * 896 + ROWS : (i + 1) * 896] = jnp.where(first, other, mine)
    return jnp.dot(left[...], right[:, :ROWS], preferred_element_type=F32)


def first_kernel(core_ref, pos_ref, *refs):
    lefts, (share_ref, right_ref, out_ref, weight_ref, left) = refs[:4], refs[4:]
    squares = jnp.zeros((), F32)
    for i in range(16):
        squares += jnp.sum(right_ref[i * SUB : i * SUB + 16, ROWS:].astype(F32)) * 0.0625
    scale = 1.0 / (jnp.sqrt(jnp.full((8, TILE), squares, F32)) + 1e-07)
    scale = jnp.max(scale)
    twice = scale * scale
    first = core_ref[0] == 0
    for i, by in enumerate((0, 1, 3, 2)):
        rows = slice(i % 2 * SUB, (i % 2 + 1) * SUB)
        mine, other = lefts[i // 2][rows, :ROWS], lefts[2 + i // 2][rows, :ROWS]
        line = jnp.concatenate([jnp.where(first, mine, other), jnp.where(first, other, mine)], 1)
        left[:, pl.ds(pl.multiple_of((pos_ref[2] ^ by) * 896, TILE), 896)] = line
    total = jnp.dot(left[...], right_ref[:, :ROWS], preferred_element_type=F32)
    total = total * twice * (coef_quintic * twice) + (coef_cubic * twice) * share_ref[:, :ROWS].astype(F32)
    out_ref[...] = total.astype(BF)
    weight_ref[0] = twice
    weight_ref[1] = coef_linear * twice
    weight_ref[2] = scale * math.sqrt(18432)


def place_kernel(pos_ref, *refs):
    place(pos_ref, refs[:8], refs[8])


def first_mul(core, pos, lefts, share, right):
    return call(
        first_kernel,
        [struct(SUB, ROWS), struct(3, dtype=F32)],
        (2, 6),
        "first_mul",
        2 * SUB * ROWS * ALL,
        [pltpu.VMEM((SUB, ALL), BF)],
        scalars_out=1,
    )(core, pos, *lefts, share, right)


def mul_kernel(weights, count, core_ref, weight_ref, mine_ref, other_ref, right_ref, *refs):
    extras, outs, left = refs[:count], refs[count:-1], refs[-1]
    if weights is None:
        weights = [weight_ref[0], weight_ref[1]]
    total = product(core_ref, mine_ref, other_ref, right_ref, left) * weights[0]
    for weight, extra in zip(weights[1:], extras):
        total += weight * extra[:, :ROWS].astype(F32)
    total = total.astype(BF)
    if len(outs) == 1:
        outs[0][...] = total
    else:
        outs[0][...] = total[:, :HALF]
        outs[1][:, :REST] = total[:, HALF:]
        outs[1][:, REST:] = jnp.zeros((SUB, HALF - REST), BF)


def mul(core, weight, lefts, right, weights, extras, halves=False, limit=VMEM):
    return call(
        functools.partial(mul_kernel, weights, len(extras)),
        [struct(SUB, HALF)] * 2 if halves else [struct(SUB, ROWS)],
        (2, 3 + len(extras)),
        "mul",
        2 * SUB * ROWS * ALL,
        [pltpu.VMEM((SUB, ALL), BF)],
        limit=limit,
    )(core, weight, *lefts, right, *extras)


def apply_kernel(weight_ref, pos_ref, upper_ref, lower_ref, panel_ref, *refs):
    parts, (out_ref, send_ref, right, mat) = refs[:8], refs[8:]
    place(pos_ref, parts, right)
    for k in range(8):
        mat[:, k * ROWS : (k + 1) * ROWS] = right[k * ROWS : (k + 1) * ROWS, :].T
    linear = coef_linear * coef_linear
    for i, own in ((0, upper_ref), (SUB, lower_ref)):
        total = jnp.dot(mat[i : i + SUB, :], panel_ref[...], preferred_element_type=F32)
        total = (total + linear * own[:SUB, :].astype(F32)) * weight_ref[2]
        out_ref[i : i + SUB, :] = total
        send_ref[i : i + SUB, :] = total.astype(BF)


def apply(weight, pos, upper, lower, panel, parts):
    return call(
        apply_kernel,
        [struct(ROWS, COLS, dtype=F32), struct(ROWS, COLS)],
        (2, 11),
        "apply",
        2 * ALL * ROWS * COLS,
        [pltpu.VMEM((ALL, ROWS), BF), pltpu.VMEM((ROWS, ALL), BF)],
    )(weight, pos, upper, lower, panel, *parts)


def gather_rows(value):
    mine = lax.all_gather(value, "z")
    return [mine, other_core(mine)]


def gather_plane(value):
    return lax.all_gather(value, PLANE, axis=0, tiled=True)


def body(momentum):
    z, c = (lax.axis_index(name).astype(jnp.int32) for name in ("z", "c"))
    same = lax.axis_index("xh") == c
    core = c.reshape(1)
    x = (lax.axis_index("xh") * 2 + lax.axis_index("xl")).astype(jnp.int32)
    y = lax.axis_index("y").astype(jnp.int32)
    pos = jnp.stack([x, y, z])

    upper, lower = (trade_roles(value) for value in cast(momentum))
    upper_1 = swap_z(upper, 1)
    lower_3 = swap_z(lower, 3)
    uppers = jnp.concatenate([upper, upper_1], 0)
    lowers = jnp.concatenate([lower, lower_3], 0)
    uppers_3 = swap_z(uppers, 3)
    lowers_1 = swap_z(lowers, 1)
    done = gram(uppers, lowers)
    near_0, near_1, uppers_3, lowers_1, done = lax.optimization_barrier((uppers, lowers, uppers_3, lowers_1, done))
    early = [uppers, lowers, uppers_3, lowers_1]
    late = [other_core(part) for part in (uppers_3, lowers_1, near_0, near_1)]
    more = gram(uppers, lowers, uppers_3, lowers_1)
    near_at, far_at = ((0, 0), (1, 0), (0, 1), (3, 1)), ((3, 0), (2, 0), (1, 1), (2, 1))
    places = [(by, 0, half) for by, half in near_at + far_at] + [(by, 1, half) for by, half in far_at + near_at]
    by, swap, half = (np.array(column, np.int32) for column in zip(*places))
    piece_x = z ^ by
    piece_y = (c ^ swap) * 2 + half
    order = piece_x * 4 + piece_y

    gray_x, gray_y = ((e ^ (e >> 1)) * 4 for e in (piece_x ^ x, piece_y ^ y))
    flip_x, flip_y = (((g & 4) * 2 + (g >> 1 & 4)) for g in (gray_x, gray_y))
    far_x, far_y = (piece_x - x) & 3, (piece_y - y) & 3
    index = jnp.concatenate([gray_y + far_x, flip_y + far_x, gray_x + far_y, flip_x + far_y])
    *split, value = gram_more(index, done, more, early, late)
    a, wide, rest = scatter_plane(split, value)
    near = jnp.concatenate([a, swap_z(a, 1)], 0)
    far = swap_z(near, 3)
    lefts = [near, far, other_core(near), other_core(far)]
    a_right = call(place_kernel, [struct(ALL, WIDE)], (1, 8), "place", 0)(pos, *gather_parts(wide, rest))[0]
    b, weight = first_mul(core, pos, lefts, a, a_right)

    b_right = gather_plane(b)
    (v,) = mul(core, weight, gather_rows(b), a_right, None, (a,))
    (a2,) = mul(core, weight, gather_rows(v), b_right, (1.0, coef_linear), (v,))

    a2_right = gather_plane(a2)
    (h,) = mul(core, weight, gather_rows(a2), b_right, (1.0, coef_linear), (a2,))
    weights = (coef_quintic, coef_cubic, coef_linear)
    wide, rest = mul(core, weight, gather_rows(h), a2_right, weights, (h, b), True, MOST)
    wide, rest, order = lax.optimization_barrier((wide, rest, order))
    panel = call(panel_kernel, [struct(16, SUB, COLS)], (1, 8), "panel", 0)(order, *early, *late)[0]
    panel = panel.reshape(ALL, COLS)

    update, sent = apply(weight, pos, upper, lower, panel, gather_parts(wide, rest))
    return jnp.where(same, update, trade_roles(sent).astype(F32))


def solution(mesh):
    split = Mesh(mesh.devices.reshape(SIZES), NAMES)
    placed = P(("z", "xh"), ("xl", "y", "c"))
    return jax.shard_map(body, mesh=split, in_specs=(placed,), out_specs=placed, check_vma=False)
```

```python
import functools
import math

import jax
import jax.numpy as jnp
import numpy as np
from jax import lax
from jax.experimental import pallas as pl
from jax.experimental.pallas import tpu as pltpu
from jax.sharding import Mesh, PartitionSpec as P

coef_linear = 3.4445
coef_cubic = -4.775
coef_quintic = 2.0315

NAMES = ("z", "xh", "xl", "y", "c")
SIZES = (4, 2, 2, 4, 2)
PLANE = ("xh", "xl", "y")
BF = jnp.bfloat16
F32 = jnp.float32
ROWS = 448
SUB = 224
TAIL = 240
COLS = 1152
ALL = 3584
TILE = 128
WIDE = 512
VMEM = 20 * 1024 * 1024
MOST = 60 * 1024 * 1024
HALF = 256
REST = ROWS - HALF

def flat(pos):
    index = 0
    for value, size in zip(pos, SIZES):
        index = index * size + value
    return index


def move(value, target):
    every = [(z, a, b, y, c) for z in range(4) for a in range(2) for b in range(2) for y in range(4) for c in range(2)]
    return lax.ppermute(value, NAMES, [(flat(pos), flat(target(*pos))) for pos in every])


def swap_z(value, by):
    return move(value, lambda z, xh, xl, y, c: (z ^ by, xh, xl, y, c))


def along_x(value, step):
    def target(z, xh, xl, y, c):
        x = (xh * 2 + xl - step) % 4
        return (z, x // 2, x % 2, y, c)

    return move(value, target)


def along_y(value, step):
    return move(value, lambda z, xh, xl, y, c: (z, xh, xl, (y - step) % 4, c))


def swap_x(value, by):
    return move(value, lambda z, xh, xl, y, c: (z, xh ^ (by >> 1), xl ^ (by & 1), y, c))


def swap_y(value, by):
    return move(value, lambda z, xh, xl, y, c: (z, xh, xl, y ^ by, c))


def other_core(value):
    return move(value, lambda z, xh, xl, y, c: (z, xh, xl, y, 1 - c))


def trade_roles(value):
    return move(value, lambda z, xh, xl, y, c: (z, c, xl, y, xh))


def struct(*shape, dtype=BF):
    return jax.ShapeDtypeStruct(shape, dtype)


def call(kernel, shapes, counts, name, flops, scratch=(), scalars_out=0, limit=VMEM):
    smem, vmem = counts
    n = len(shapes)
    return pl.pallas_call(
        kernel,
        out_shape=shapes,
        in_specs=[pl.BlockSpec(memory_space=pltpu.SMEM)] * smem + [pl.BlockSpec(memory_space=pltpu.VMEM)] * vmem,
        out_specs=[pl.BlockSpec(memory_space=pltpu.VMEM)] * (n - scalars_out)
        + [pl.BlockSpec(memory_space=pltpu.SMEM)] * scalars_out,
        scratch_shapes=list(scratch),
        compiler_params=pltpu.CompilerParams(vmem_limit_bytes=limit),
        cost_estimate=pl.CostEstimate(flops=flops, bytes_accessed=6 << 20, transcendentals=0),
        name=name,
    )


def split_value(value):
    lane = lax.broadcasted_iota(jnp.int32, (16, TILE), 1)
    whole = jnp.full((16, TILE), value, F32)
    high = whole.astype(BF).astype(F32)
    middle = (whole - high).astype(BF).astype(F32)
    low = whole - high - middle
    out = jnp.where(lane == 0, high, jnp.where(lane == 1, middle, jnp.where(lane == 2, low, 0.0)))
    return out.astype(BF)


def cast_kernel(in_ref, upper_ref, lower_ref):
    squares = jnp.zeros((8, COLS), F32)
    for i in range(0, ROWS, 32):
        block = in_ref[i : i + 32, :]
        if i < SUB:
            upper_ref[i : i + 32, :] = block.astype(BF)
        else:
            lower_ref[i - SUB : i - SUB + 32, :] = block.astype(BF)
        square = block * block
        squares += (square[:8] + square[8:16]) + (square[16:24] + square[24:])
    lower_ref[SUB:, :] = jnp.zeros((TAIL - SUB, COLS), BF)
    lower_ref[SUB:, :TILE] = split_value(jnp.sum(squares))


def cast(momentum):
    return call(cast_kernel, [struct(SUB, COLS), struct(TAIL, COLS)], (0, 1), "cast", 0)(momentum)


def pieces(refs):
    for ref in refs:
        step = ref.shape[0] // 2
        for i in range(2):
            yield ref[i * step : i * step + SUB, :]


def sum_of_squares(refs):
    total = jnp.zeros((), F32)
    for ref in refs:
        if ref.shape[0] == 2 * TAIL:
            for i in range(2):
                total += jnp.sum(ref[i * TAIL + SUB : (i + 1) * TAIL, :TILE].astype(F32)) * 0.0625
    return total


def turn(upper_ref, lower_ref, turned):
    turned[:, :SUB] = upper_ref[:SUB, :].T
    turned[:, SUB:] = lower_ref[:SUB, :].T


def gram_kernel(upper_ref, lower_ref, *refs):
    parts, out_ref, turned = refs[:-2], refs[-2], refs[-1]
    turn(upper_ref, lower_ref, turned)
    for i, piece in enumerate(pieces(parts or (upper_ref, lower_ref))):
        out_ref[i] = jnp.dot(piece, turned[...], preferred_element_type=F32).astype(BF)


def gram(*parts):
    scratch = [pltpu.VMEM((COLS, ROWS), BF)]
    flops = 2 * 4 * SUB * ROWS * COLS
    return call(gram_kernel, [struct(4, SUB, ROWS)], (0, len(parts)), "gram", flops, scratch)(*parts)[0]


def gram_more_kernel(count, index_ref, done_ref, more_ref, *refs):
    parts, fresh, outs = refs[:count], refs[count : 2 * count], refs[2 * count : 2 * count + 8]
    value_ref, turned, full = refs[2 * count + 8], refs[2 * count + 9], refs[2 * count + 10 :]
    turn(parts[0], parts[1], turned)

    def store(n, block):
        for q in range(4):
            end = min(TILE, ROWS - q * TILE)
            full[q][index_ref[q * 16 + n], :, :end] = block[:, q * TILE : q * TILE + end]

    for n in range(4):
        store(n, done_ref[n])
        store(4 + n, more_ref[n])
    for n, piece in enumerate(pieces(fresh)):
        store(2 * count + n, jnp.dot(piece, turned[...], preferred_element_type=F32).astype(BF))
    for q in range(4):
        end = min(TILE, ROWS - q * TILE)
        for half in range(2):
            outs[2 * q + half][:, :, :end] = full[q][half * 8 : half * 8 + 8, :, :end]
            if end < TILE:
                outs[2 * q + half][:, :, end:] = jnp.zeros((8, SUB, TILE - end), BF)
    value_ref[0] = sum_of_squares(parts) + sum_of_squares(fresh)


def gram_more(index, done, more, parts, fresh):
    count = len(parts)
    return call(
        functools.partial(gram_more_kernel, count),
        [struct(8, SUB, TILE)] * 8 + [struct(1, dtype=F32)],
        (1, 2 + 2 * count),
        "gram",
        2 * 2 * count * SUB * ROWS * COLS,
        [pltpu.VMEM((COLS, ROWS), BF)] + [pltpu.VMEM((16, SUB, TILE), BF)] * 4,
        scalars_out=1,
    )(index, done, more, *parts, *fresh)


def panel_kernel(order_ref, *refs):
    parts, out_ref = refs[:-1], refs[-1]
    for i, piece in enumerate(pieces(parts)):
        out_ref[order_ref[i]] = piece


def halve_kernel(*refs):
    keep, got, outs = refs[:4], refs[4:8], refs[8:]
    for q in range(4):
        for i in range(8):
            total = keep[q][i].astype(F32) + got[q][i].astype(F32)
            outs[2 * q + i // 4][i % 4] = total.astype(BF)


def unstack_kernel(*refs):
    keep, got, outs = refs[:4], refs[4:8], refs[8:]
    for q in range(4):
        at = (q % 2) * TILE
        for i in range(4):
            total = keep[q][i].astype(F32) + got[q][i].astype(F32)
            outs[(q // 2) * 4 + i][:, at : at + TILE] = total.astype(BF)


def sum_kernel(value_ref, *refs):
    wides, rests, (out_ref, wide_ref, rest_ref) = refs[:4], refs[4:8], refs[8:]
    for refs, sum_ref in ((wides, wide_ref), (rests, rest_ref)):
        total = refs[0][...].astype(F32)
        for ref in refs[1:]:
            total += ref[...].astype(F32)
        sum_ref[...] = total.astype(BF)
    rest_ref[:16, REST:] = split_value(value_ref[0])[:, : HALF - REST]
    out_ref[:, :HALF] = wide_ref[...]
    out_ref[:, HALF:] = rest_ref[...]


def scatter_plane(split, value):
    keep, send = split[0::2], split[1::2]
    got = [swap_y(send[0], 3), swap_y(send[1], 1), swap_x(send[2], 3), swap_x(send[3], 1)]
    split = call(halve_kernel, [struct(4, SUB, TILE)] * 8, (0, 8), "halve", 0)(*keep, *got)
    keep, send = split[0::2], split[1::2]
    got = [swap_y(send[0], 1), swap_y(send[1], 3), swap_x(send[2], 1), swap_x(send[3], 3)]
    halves = call(unstack_kernel, [struct(SUB, HALF)] * 8, (0, 8), "unstack", 0)(*keep, *got)
    wides = [halves[0]] + [along_x(halves[s], -s) for s in (1, 2, 3)]
    rests = [halves[4]] + [along_y(halves[4 + s], -s) for s in (1, 2, 3)]
    shapes = [struct(SUB, WIDE), struct(SUB, HALF), struct(SUB, HALF)]
    return call(sum_kernel, shapes, (1, 8), "sum", 0)(value, *wides, *rests)


def stack_kernel(*refs):
    for n, outs in ((0, refs[8:10]), (4, refs[10:12])):
        for i in range(4):
            outs[0][i] = refs[n + i][:, :TILE]
            outs[1][i] = refs[n + i][:, TILE:]


def join_kernel(*refs):
    mine, got, outs = refs[:4], refs[4:8], refs[8:]
    for q in range(4):
        outs[q][:4] = mine[q][...]
        outs[q][4:] = got[q][...]


def gather_parts(wide, rest):
    wides = [wide] + [along_x(wide, s) for s in (1, 2, 3)]
    rests = [rest] + [along_y(rest, s) for s in (1, 2, 3)]
    parts = call(stack_kernel, [struct(4, SUB, TILE)] * 4, (0, 8), "stack", 0)(*wides, *rests)
    got = [swap_y(parts[0], 1), swap_y(parts[1], 3), swap_x(parts[2], 1), swap_x(parts[3], 3)]
    parts = call(join_kernel, [struct(8, SUB, TILE)] * 4, (0, 8), "join", 0)(*parts, *got)
    got = [swap_y(parts[0], 3), swap_y(parts[1], 1), swap_x(parts[2], 3), swap_x(parts[3], 1)]
    return [*parts, *got]


def place(pos_ref, refs, right, first=0):
    x, y = pos_ref[0], pos_ref[1]
    for q in range(first, first + len(refs) // 2):
        at = (q - first) * TILE
        end = min(TILE, right.shape[1] - at)
        near, far = ((1, 3), (3, 1))[q % 2]
        for i in range(16):
            by = (0, near, far, near ^ far)[i // 4]
            if q < 2:
                share = lax.rem(x + i % 4, 4) * 4 + (y ^ by)
            else:
                share = (x ^ by) * 4 + lax.rem(y + i % 4, 4)
            rows = pl.ds(pl.multiple_of(share * SUB, SUB), SUB)
            right[rows, at : at + end] = refs[q - first + (i // 8) * (len(refs) // 2)][i % 8, :, :end]


def product(core_ref, mine_ref, other_ref, right, left):
    first = core_ref[0] == 0
    for i in range(4):
        mine, other = mine_ref[i, :, :ROWS], other_ref[i, :, :ROWS]
        left[:, i * 896 : i * 896 + ROWS] = jnp.where(first, mine, other)
        left[:, i * 896 + ROWS : (i + 1) * 896] = jnp.where(first, other, mine)
    return jnp.dot(left[...], right[:, :ROWS], preferred_element_type=F32)


def first_kernel(core_ref, pos_ref, *refs):
    lefts, (share_ref, right_ref, out_ref, weight_ref, left) = refs[:4], refs[4:]
    squares = jnp.zeros((), F32)
    for i in range(16):
        squares += jnp.sum(right_ref[i * SUB : i * SUB + 16, ROWS:].astype(F32)) * 0.0625
    scale = 1.0 / (jnp.sqrt(jnp.full((8, TILE), squares, F32)) + 1e-07)
    scale = jnp.max(scale)
    twice = scale * scale
    first = core_ref[0] == 0
    for i, by in enumerate((0, 1, 3, 2)):
        rows = slice(i % 2 * SUB, (i % 2 + 1) * SUB)
        mine, other = lefts[i // 2][rows, :ROWS], lefts[2 + i // 2][rows, :ROWS]
        line = jnp.concatenate([jnp.where(first, mine, other), jnp.where(first, other, mine)], 1)
        left[:, pl.ds(pl.multiple_of((pos_ref[2] ^ by) * 896, TILE), 896)] = line
    total = jnp.dot(left[...], right_ref[:, :ROWS], preferred_element_type=F32)
    total = total * twice * (coef_quintic * twice) + (coef_cubic * twice) * share_ref[:, :ROWS].astype(F32)
    out_ref[...] = total.astype(BF)
    weight_ref[0] = twice
    weight_ref[1] = coef_linear * twice
    weight_ref[2] = scale * math.sqrt(18432)


def place_kernel(pos_ref, *refs):
    place(pos_ref, refs[:8], refs[8])


def first_mul(core, pos, lefts, share, right):
    return call(
        first_kernel,
        [struct(SUB, ROWS), struct(3, dtype=F32)],
        (2, 6),
        "first_mul",
        2 * SUB * ROWS * ALL,
        [pltpu.VMEM((SUB, ALL), BF)],
        scalars_out=1,
    )(core, pos, *lefts, share, right)


def mul_kernel(weights, count, core_ref, weight_ref, mine_ref, other_ref, right_ref, *refs):
    extras, outs, left = refs[:count], refs[count:-1], refs[-1]
    if weights is None:
        weights = [weight_ref[0], weight_ref[1]]
    total = product(core_ref, mine_ref, other_ref, right_ref, left) * weights[0]
    for weight, extra in zip(weights[1:], extras):
        total += weight * extra[:, :ROWS].astype(F32)
    total = total.astype(BF)
    if len(outs) == 1:
        outs[0][...] = total
    else:
        outs[0][...] = total[:, :HALF]
        outs[1][:, :REST] = total[:, HALF:]
        outs[1][:, REST:] = jnp.zeros((SUB, HALF - REST), BF)


def mul(core, weight, lefts, right, weights, extras, halves=False, limit=VMEM):
    return call(
        functools.partial(mul_kernel, weights, len(extras)),
        [struct(SUB, HALF)] * 2 if halves else [struct(SUB, ROWS)],
        (2, 3 + len(extras)),
        "mul",
        2 * SUB * ROWS * ALL,
        [pltpu.VMEM((SUB, ALL), BF)],
        limit=limit,
    )(core, weight, *lefts, right, *extras)


def own_rows(upper_ref, lower_ref, first, end):
    for base, ref in ((0, upper_ref), (SUB, lower_ref)):
        low, high = max(first, base), min(end, base + SUB)
        if low < high:
            yield low - first, ref[low - base : high - base, :]


def apply_kernel(first, weight_ref, pos_ref, upper_ref, lower_ref, panel_ref, *refs):
    parts, (out_ref, send_ref, right, mat) = refs[:4], refs[4:]
    rows = out_ref.shape[0]
    place(pos_ref, parts, right, first // TILE)
    for k in range(4):
        mat[:, k * 896 : (k + 1) * 896] = right[k * 896 : (k + 1) * 896, :].T
    total = jnp.dot(mat[...], panel_ref[...], preferred_element_type=F32)
    linear = coef_linear * coef_linear
    for at, own in own_rows(upper_ref, lower_ref, first, first + rows):
        some = slice(at, at + own.shape[0])
        result = (total[some, :] + linear * own.astype(F32)) * weight_ref[2]
        out_ref[some, :] = result
        send_ref[some, :] = result.astype(BF)


def apply(first, rows, weight, pos, upper, lower, panel, parts):
    return call(
        functools.partial(apply_kernel, first),
        [struct(rows, COLS, dtype=F32), struct(rows, COLS)],
        (2, 7),
        "apply",
        2 * ALL * rows * COLS,
        [pltpu.VMEM((ALL, rows), BF), pltpu.VMEM((rows, ALL), BF)],
    )(weight, pos, upper, lower, panel, *parts)


def gather_rows(value):
    mine = lax.all_gather(value, "z")
    return [mine, other_core(mine)]


def gather_plane(value):
    return lax.all_gather(value, PLANE, axis=0, tiled=True)


def body(momentum):
    z, c = (lax.axis_index(name).astype(jnp.int32) for name in ("z", "c"))
    same = lax.axis_index("xh") == c
    core = c.reshape(1)
    x = (lax.axis_index("xh") * 2 + lax.axis_index("xl")).astype(jnp.int32)
    y = lax.axis_index("y").astype(jnp.int32)
    pos = jnp.stack([x, y, z])

    upper, lower = (trade_roles(value) for value in cast(momentum))
    upper_1 = swap_z(upper, 1)
    lower_3 = swap_z(lower, 3)
    uppers = jnp.concatenate([upper, upper_1], 0)
    lowers = jnp.concatenate([lower, lower_3], 0)
    uppers_3 = swap_z(uppers, 3)
    lowers_1 = swap_z(lowers, 1)
    done = gram(uppers, lowers)
    near_0, near_1, uppers_3, lowers_1, done = lax.optimization_barrier((uppers, lowers, uppers_3, lowers_1, done))
    early = [uppers, lowers, uppers_3, lowers_1]
    late = [other_core(part) for part in (uppers_3, lowers_1, near_0, near_1)]
    more = gram(uppers, lowers, uppers_3, lowers_1)
    near_at, far_at = ((0, 0), (1, 0), (0, 1), (3, 1)), ((3, 0), (2, 0), (1, 1), (2, 1))
    places = [(by, 0, half) for by, half in near_at + far_at] + [(by, 1, half) for by, half in far_at + near_at]
    by, swap, half = (np.array(column, np.int32) for column in zip(*places))
    piece_x = z ^ by
    piece_y = (c ^ swap) * 2 + half
    order = piece_x * 4 + piece_y

    gray_x, gray_y = ((e ^ (e >> 1)) * 4 for e in (piece_x ^ x, piece_y ^ y))
    flip_x, flip_y = (((g & 4) * 2 + (g >> 1 & 4)) for g in (gray_x, gray_y))
    far_x, far_y = (piece_x - x) & 3, (piece_y - y) & 3
    index = jnp.concatenate([gray_y + far_x, flip_y + far_x, gray_x + far_y, flip_x + far_y])
    *split, value = gram_more(index, done, more, early, late)
    a, wide, rest = scatter_plane(split, value)
    near = jnp.concatenate([a, swap_z(a, 1)], 0)
    far = swap_z(near, 3)
    lefts = [near, far, other_core(near), other_core(far)]
    a_right = call(place_kernel, [struct(ALL, WIDE)], (1, 8), "place", 0)(pos, *gather_parts(wide, rest))[0]
    b, weight = first_mul(core, pos, lefts, a, a_right)

    b_right = gather_plane(b)
    (v,) = mul(core, weight, gather_rows(b), a_right, None, (a,))
    (a2,) = mul(core, weight, gather_rows(v), b_right, (1.0, coef_linear), (v,), limit=MOST)

    a2_right = gather_plane(a2)
    (h,) = mul(core, weight, gather_rows(a2), b_right, (1.0, coef_linear), (a2,))
    weights = (coef_quintic, coef_cubic, coef_linear)
    wide, rest = mul(core, weight, gather_rows(h), a2_right, weights, (h, b), halves=True, limit=MOST)
    wide, rest, order = lax.optimization_barrier((wide, rest, order))
    panel = call(panel_kernel, [struct(16, SUB, COLS)], (1, 8), "panel", 0)(order, *early, *late)[0]
    panel = panel.reshape(ALL, COLS)

    parts = gather_parts(wide, rest)
    head, sent_head = apply(0, HALF, weight, pos, upper, lower, panel, parts[:2] + parts[4:6])
    sent_head = trade_roles(sent_head)
    tail, sent_tail = apply(HALF, REST, weight, pos, upper, lower, panel, parts[2:4] + parts[6:])
    sent_tail = trade_roles(sent_tail)
    both = ((head, sent_head), (tail, sent_tail))
    return jnp.concatenate([jnp.where(same, kept, sent.astype(F32)) for kept, sent in both], 0)


def solution(mesh):
    split = Mesh(mesh.devices.reshape(SIZES), NAMES)
    placed = P(("z", "xh"), ("xl", "y", "c"))
    return jax.shard_map(body, mesh=split, in_specs=(placed,), out_specs=placed, check_vma=False)
```

```python
import functools
import math

import jax
import jax.numpy as jnp
import numpy as np
from jax import lax
from jax.experimental import pallas as pl
from jax.experimental.pallas import tpu as pltpu
from jax.sharding import Mesh, PartitionSpec as P

coef_linear = 3.4445
coef_cubic = -4.775
coef_quintic = 2.0315

NAMES = ("z", "xh", "xl", "y", "c")
SIZES = (4, 2, 2, 4, 2)
PLANE = ("xh", "xl", "y")
BF = jnp.bfloat16
F32 = jnp.float32
ROWS = 448
SUB = 224
TAIL = 240
COLS = 1152
ALL = 3584
TILE = 128
WIDE = 512
VMEM = 20 * 1024 * 1024
MOST = 60 * 1024 * 1024
HALF = 256
REST = ROWS - HALF

def flat(pos):
    index = 0
    for value, size in zip(pos, SIZES):
        index = index * size + value
    return index


def move(value, target):
    every = [(z, a, b, y, c) for z in range(4) for a in range(2) for b in range(2) for y in range(4) for c in range(2)]
    return lax.ppermute(value, NAMES, [(flat(pos), flat(target(*pos))) for pos in every])


def swap_z(value, by):
    return move(value, lambda z, xh, xl, y, c: (z ^ by, xh, xl, y, c))


def along_x(value, step):
    def target(z, xh, xl, y, c):
        x = (xh * 2 + xl - step) % 4
        return (z, x // 2, x % 2, y, c)

    return move(value, target)


def along_y(value, step):
    return move(value, lambda z, xh, xl, y, c: (z, xh, xl, (y - step) % 4, c))


def swap_x(value, by):
    return move(value, lambda z, xh, xl, y, c: (z, xh ^ (by >> 1), xl ^ (by & 1), y, c))


def swap_y(value, by):
    return move(value, lambda z, xh, xl, y, c: (z, xh, xl, y ^ by, c))


def other_core(value):
    return move(value, lambda z, xh, xl, y, c: (z, xh, xl, y, 1 - c))


def trade_roles(value):
    return move(value, lambda z, xh, xl, y, c: (z, c, xl, y, xh))


def struct(*shape, dtype=BF):
    return jax.ShapeDtypeStruct(shape, dtype)


def call(kernel, shapes, counts, name, flops, scratch=(), scalars_out=0, limit=VMEM):
    smem, vmem = counts
    n = len(shapes)
    return pl.pallas_call(
        kernel,
        out_shape=shapes,
        in_specs=[pl.BlockSpec(memory_space=pltpu.SMEM)] * smem + [pl.BlockSpec(memory_space=pltpu.VMEM)] * vmem,
        out_specs=[pl.BlockSpec(memory_space=pltpu.VMEM)] * (n - scalars_out)
        + [pl.BlockSpec(memory_space=pltpu.SMEM)] * scalars_out,
        scratch_shapes=list(scratch),
        compiler_params=pltpu.CompilerParams(vmem_limit_bytes=limit),
        cost_estimate=pl.CostEstimate(flops=flops, bytes_accessed=6 << 20, transcendentals=0),
        name=name,
    )


def split_value(value):
    lane = lax.broadcasted_iota(jnp.int32, (16, TILE), 1)
    whole = jnp.full((16, TILE), value, F32)
    high = whole.astype(BF).astype(F32)
    middle = (whole - high).astype(BF).astype(F32)
    low = whole - high - middle
    out = jnp.where(lane == 0, high, jnp.where(lane == 1, middle, jnp.where(lane == 2, low, 0.0)))
    return out.astype(BF)


def cast_kernel(in_ref, upper_ref, lower_ref):
    squares = jnp.zeros((8, COLS), F32)
    for i in range(0, ROWS, 32):
        block = in_ref[i : i + 32, :]
        if i < SUB:
            upper_ref[i : i + 32, :] = block.astype(BF)
        else:
            lower_ref[i - SUB : i - SUB + 32, :] = block.astype(BF)
        square = block * block
        squares += (square[:8] + square[8:16]) + (square[16:24] + square[24:])
    lower_ref[SUB:, :] = jnp.zeros((TAIL - SUB, COLS), BF)
    lower_ref[SUB:, :TILE] = split_value(jnp.sum(squares))


def cast(momentum):
    return call(cast_kernel, [struct(SUB, COLS), struct(TAIL, COLS)], (0, 1), "cast", 0)(momentum)


def pieces(refs):
    for ref in refs:
        step = ref.shape[0] // 2
        for i in range(2):
            yield ref[i * step : i * step + SUB, :]


def sum_of_squares(refs):
    total = jnp.zeros((16, TILE), F32)
    for ref in refs:
        if ref.shape[0] == 2 * TAIL:
            for i in range(2):
                total += ref[i * TAIL + SUB : (i + 1) * TAIL, :TILE].astype(F32)
    return jnp.sum(total) * 0.0625


def turn(upper_ref, lower_ref, turned):
    turned[:, :SUB] = upper_ref[:SUB, :].T
    turned[:, SUB:] = lower_ref[:SUB, :].T


def gram_kernel(upper_ref, lower_ref, *refs):
    parts, out_ref, turned = refs[:-2], refs[-2], refs[-1]
    turn(upper_ref, lower_ref, turned)
    for i, piece in enumerate(pieces(parts or (upper_ref, lower_ref))):
        out_ref[i] = jnp.dot(piece, turned[...], preferred_element_type=F32).astype(BF)


def gram(*parts):
    scratch = [pltpu.VMEM((COLS, ROWS), BF)]
    flops = 2 * 4 * SUB * ROWS * COLS
    return call(gram_kernel, [struct(4, SUB, ROWS)], (0, len(parts)), "gram", flops, scratch)(*parts)[0]


def gram_more_kernel(count, index_ref, done_ref, more_ref, *refs):
    parts, fresh, outs = refs[:count], refs[count : 2 * count], refs[2 * count : 2 * count + 8]
    value_ref, turned, full = refs[2 * count + 8], refs[2 * count + 9], refs[2 * count + 10 :]
    turn(parts[0], parts[1], turned)

    def store(n, block):
        for q in range(4):
            end = min(TILE, ROWS - q * TILE)
            full[q][index_ref[q * 16 + n], :, :end] = block[:, q * TILE : q * TILE + end]

    for n in range(4):
        store(n, done_ref[n])
        store(4 + n, more_ref[n])
    for n, piece in enumerate(pieces(fresh)):
        store(2 * count + n, jnp.dot(piece, turned[...], preferred_element_type=F32).astype(BF))
    for q in range(4):
        end = min(TILE, ROWS - q * TILE)
        for half in range(2):
            outs[2 * q + half][:, :, :end] = full[q][half * 8 : half * 8 + 8, :, :end]
            if end < TILE:
                outs[2 * q + half][:, :, end:] = jnp.zeros((8, SUB, TILE - end), BF)
    value_ref[0] = sum_of_squares(refs[: 2 * count])


def gram_more(index, done, more, parts, fresh):
    count = len(parts)
    return call(
        functools.partial(gram_more_kernel, count),
        [struct(8, SUB, TILE)] * 8 + [struct(1, dtype=F32)],
        (1, 2 + 2 * count),
        "gram",
        2 * 2 * count * SUB * ROWS * COLS,
        [pltpu.VMEM((COLS, ROWS), BF)] + [pltpu.VMEM((16, SUB, TILE), BF)] * 4,
        scalars_out=1,
    )(index, done, more, *parts, *fresh)


def panel_kernel(order_ref, *refs):
    parts, out_ref = refs[:-1], refs[-1]
    for i, piece in enumerate(pieces(parts)):
        out_ref[order_ref[i]] = piece


def halve_kernel(*refs):
    keep, got, outs = refs[:4], refs[4:8], refs[8:]
    for q in range(4):
        for i in range(8):
            total = keep[q][i].astype(F32) + got[q][i].astype(F32)
            outs[2 * q + i // 4][i % 4] = total.astype(BF)


def unstack_kernel(*refs):
    keep, got, outs = refs[:4], refs[4:8], refs[8:]
    for q in range(4):
        at = (q % 2) * TILE
        for i in range(4):
            total = keep[q][i].astype(F32) + got[q][i].astype(F32)
            outs[(q // 2) * 4 + i][:, at : at + TILE] = total.astype(BF)


def sum_kernel(value_ref, *refs):
    wides, rests, (out_ref, wide_ref, rest_ref) = refs[:4], refs[4:8], refs[8:]
    for refs, sum_ref in ((wides, wide_ref), (rests, rest_ref)):
        total = refs[0][...].astype(F32)
        for ref in refs[1:]:
            total += ref[...].astype(F32)
        sum_ref[...] = total.astype(BF)
    rest_ref[:16, REST:] = split_value(value_ref[0])[:, : HALF - REST]
    out_ref[:, :HALF] = wide_ref[...]
    out_ref[:, HALF:] = rest_ref[...]


def scatter_plane(split, value):
    keep, send = split[0::2], split[1::2]
    got = [swap_y(send[0], 3), swap_y(send[1], 1), swap_x(send[2], 3), swap_x(send[3], 1)]
    split = call(halve_kernel, [struct(4, SUB, TILE)] * 8, (0, 8), "halve", 0)(*keep, *got)
    keep, send = split[0::2], split[1::2]
    got = [swap_y(send[0], 1), swap_y(send[1], 3), swap_x(send[2], 1), swap_x(send[3], 3)]
    halves = call(unstack_kernel, [struct(SUB, HALF)] * 8, (0, 8), "unstack", 0)(*keep, *got)
    wides = [halves[0]] + [along_x(halves[s], -s) for s in (1, 2, 3)]
    rests = [halves[4]] + [along_y(halves[4 + s], -s) for s in (1, 2, 3)]
    shapes = [struct(SUB, WIDE), struct(SUB, HALF), struct(SUB, HALF)]
    return call(sum_kernel, shapes, (1, 8), "sum", 0)(value, *wides, *rests)


def stack_kernel(*refs):
    for n, outs in ((0, refs[8:10]), (4, refs[10:12])):
        for i in range(4):
            outs[0][i] = refs[n + i][:, :TILE]
            outs[1][i] = refs[n + i][:, TILE:]


def join_kernel(*refs):
    mine, got, outs = refs[:4], refs[4:8], refs[8:]
    for q in range(4):
        outs[q][:4] = mine[q][...]
        outs[q][4:] = got[q][...]


def gather_parts(wide, rest):
    wides = [wide] + [along_x(wide, s) for s in (1, 2, 3)]
    rests = [rest] + [along_y(rest, s) for s in (1, 2, 3)]
    parts = call(stack_kernel, [struct(4, SUB, TILE)] * 4, (0, 8), "stack", 0)(*wides, *rests)
    got = [swap_y(parts[0], 1), swap_y(parts[1], 3), swap_x(parts[2], 1), swap_x(parts[3], 3)]
    parts = call(join_kernel, [struct(8, SUB, TILE)] * 4, (0, 8), "join", 0)(*parts, *got)
    got = [swap_y(parts[0], 3), swap_y(parts[1], 1), swap_x(parts[2], 3), swap_x(parts[3], 1)]
    return [*parts, *got]


def place(pos_ref, refs, right, first=0):
    x, y = pos_ref[0], pos_ref[1]
    for q in range(first, first + len(refs) // 2):
        at = (q - first) * TILE
        end = min(TILE, right.shape[1] - at)
        near, far = ((1, 3), (3, 1))[q % 2]
        for i in range(16):
            by = (0, near, far, near ^ far)[i // 4]
            if q < 2:
                share = lax.rem(x + i % 4, 4) * 4 + (y ^ by)
            else:
                share = (x ^ by) * 4 + lax.rem(y + i % 4, 4)
            rows = pl.ds(pl.multiple_of(share * SUB, SUB), SUB)
            right[rows, at : at + end] = refs[q - first + (i // 8) * (len(refs) // 2)][i % 8, :, :end]


def product(core_ref, mine_ref, other_ref, right, left):
    first = core_ref[0] == 0
    for i in range(4):
        mine, other = mine_ref[i, :, :ROWS], other_ref[i, :, :ROWS]
        left[:, i * 896 : i * 896 + ROWS] = jnp.where(first, mine, other)
        left[:, i * 896 + ROWS : (i + 1) * 896] = jnp.where(first, other, mine)
    return jnp.dot(left[...], right[:, :ROWS], preferred_element_type=F32)


def first_kernel(core_ref, pos_ref, *refs):
    lefts, (share_ref, right_ref, out_ref, weight_ref, left) = refs[:4], refs[4:]
    squares = jnp.zeros((16, WIDE - ROWS), F32)
    for i in range(16):
        squares += right_ref[i * SUB : i * SUB + 16, ROWS:].astype(F32)
    squares = jnp.sum(squares) * 0.0625
    scale = 1.0 / (jnp.sqrt(jnp.full((8, TILE), squares, F32)) + 1e-07)
    scale = jnp.max(scale)
    twice = scale * scale
    first = core_ref[0] == 0
    for i, by in enumerate((0, 1, 3, 2)):
        rows = slice(i % 2 * SUB, (i % 2 + 1) * SUB)
        mine, other = lefts[i // 2][rows, :ROWS], lefts[2 + i // 2][rows, :ROWS]
        line = jnp.concatenate([jnp.where(first, mine, other), jnp.where(first, other, mine)], 1)
        left[:, pl.ds(pl.multiple_of((pos_ref[2] ^ by) * 896, TILE), 896)] = line
    total = jnp.dot(left[...], right_ref[:, :ROWS], preferred_element_type=F32)
    total = total * twice * (coef_quintic * twice) + (coef_cubic * twice) * share_ref[:, :ROWS].astype(F32)
    out_ref[...] = total.astype(BF)
    weight_ref[0] = twice
    weight_ref[1] = coef_linear * twice
    weight_ref[2] = scale * math.sqrt(18432)


def place_kernel(pos_ref, *refs):
    place(pos_ref, refs[:8], refs[8])


def first_mul(core, pos, lefts, share, right):
    return call(
        first_kernel,
        [struct(SUB, ROWS), struct(3, dtype=F32)],
        (2, 6),
        "first_mul",
        2 * SUB * ROWS * ALL,
        [pltpu.VMEM((SUB, ALL), BF)],
        scalars_out=1,
    )(core, pos, *lefts, share, right)


def mul_kernel(weights, count, core_ref, weight_ref, mine_ref, other_ref, right_ref, *refs):
    extras, outs, left = refs[:count], refs[count:-1], refs[-1]
    if weights is None:
        weights = [weight_ref[0], weight_ref[1]]
    total = product(core_ref, mine_ref, other_ref, right_ref, left) * weights[0]
    for weight, extra in zip(weights[1:], extras):
        total += weight * extra[:, :ROWS].astype(F32)
    total = total.astype(BF)
    if len(outs) == 1:
        outs[0][...] = total
    else:
        outs[0][...] = total[:, :HALF]
        outs[1][:, :REST] = total[:, HALF:]
        outs[1][:, REST:] = jnp.zeros((SUB, HALF - REST), BF)


def mul(core, weight, lefts, right, weights, extras, halves=False, limit=VMEM):
    return call(
        functools.partial(mul_kernel, weights, len(extras)),
        [struct(SUB, HALF)] * 2 if halves else [struct(SUB, ROWS)],
        (2, 3 + len(extras)),
        "mul",
        2 * SUB * ROWS * ALL,
        [pltpu.VMEM((SUB, ALL), BF)],
        limit=limit,
    )(core, weight, *lefts, right, *extras)


def own_rows(upper_ref, lower_ref, first, end):
    for base, ref in ((0, upper_ref), (SUB, lower_ref)):
        low, high = max(first, base), min(end, base + SUB)
        if low < high:
            yield low - first, ref[low - base : high - base, :]


def apply_kernel(first, weight_ref, pos_ref, upper_ref, lower_ref, panel_ref, *refs):
    parts, (out_ref, right, mat) = refs[:4], refs[4:]
    rows = out_ref.shape[0]
    place(pos_ref, parts, right, first // TILE)
    for k in range(4):
        mat[:, k * 896 : (k + 1) * 896] = right[k * 896 : (k + 1) * 896, :].T
    total = jnp.dot(mat[...], panel_ref[...], preferred_element_type=F32)
    linear = coef_linear * coef_linear
    for at, own in own_rows(upper_ref, lower_ref, first, first + rows):
        some = slice(at, at + own.shape[0])
        result = (total[some, :] + linear * own.astype(F32)) * weight_ref[2]
        out_ref[some, :] = result.astype(BF)


def apply(first, rows, weight, pos, upper, lower, panel, parts):
    return call(
        functools.partial(apply_kernel, first),
        [struct(rows, COLS)],
        (2, 7),
        "apply",
        2 * ALL * rows * COLS,
        [pltpu.VMEM((ALL, rows), BF), pltpu.VMEM((rows, ALL), BF)],
    )(weight, pos, upper, lower, panel, *parts)[0]


def gather_rows(value):
    mine = lax.all_gather(value, "z")
    return [mine, other_core(mine)]


def gather_plane(value):
    return lax.all_gather(value, PLANE, axis=0, tiled=True)


def body(momentum):
    z, c = (lax.axis_index(name).astype(jnp.int32) for name in ("z", "c"))
    core = c.reshape(1)
    x = (lax.axis_index("xh") * 2 + lax.axis_index("xl")).astype(jnp.int32)
    y = lax.axis_index("y").astype(jnp.int32)
    pos = jnp.stack([x, y, z])

    upper, lower = (trade_roles(value) for value in cast(momentum))
    upper_1 = swap_z(upper, 1)
    lower_3 = swap_z(lower, 3)
    uppers = jnp.concatenate([upper, upper_1], 0)
    lowers = jnp.concatenate([lower, lower_3], 0)
    uppers_3 = swap_z(uppers, 3)
    lowers_1 = swap_z(lowers, 1)
    done = gram(uppers, lowers)
    near_0, near_1, uppers_3, lowers_1, done = lax.optimization_barrier((uppers, lowers, uppers_3, lowers_1, done))
    early = [uppers, lowers, uppers_3, lowers_1]
    late = [other_core(part) for part in (uppers_3, lowers_1, near_0, near_1)]
    more = gram(uppers, lowers, uppers_3, lowers_1)
    near_at, far_at = ((0, 0), (1, 0), (0, 1), (3, 1)), ((3, 0), (2, 0), (1, 1), (2, 1))
    places = [(by, 0, half) for by, half in near_at + far_at] + [(by, 1, half) for by, half in far_at + near_at]
    by, swap, half = (np.array(column, np.int32) for column in zip(*places))
    piece_x = z ^ by
    piece_y = (c ^ swap) * 2 + half
    order = piece_x * 4 + piece_y

    gray_x, gray_y = ((e ^ (e >> 1)) * 4 for e in (piece_x ^ x, piece_y ^ y))
    flip_x, flip_y = (((g & 4) * 2 + (g >> 1 & 4)) for g in (gray_x, gray_y))
    far_x, far_y = (piece_x - x) & 3, (piece_y - y) & 3
    index = jnp.concatenate([gray_y + far_x, flip_y + far_x, gray_x + far_y, flip_x + far_y])
    *split, value = gram_more(index, done, more, early, late)
    a, wide, rest = scatter_plane(split, value)
    near = jnp.concatenate([a, swap_z(a, 1)], 0)
    far = swap_z(near, 3)
    lefts = [near, far, other_core(near), other_core(far)]
    a_right = call(place_kernel, [struct(ALL, WIDE)], (1, 8), "place", 0)(pos, *gather_parts(wide, rest))[0]
    b, weight = first_mul(core, pos, lefts, a, a_right)

    b_right = gather_plane(b)
    (v,) = mul(core, weight, gather_rows(b), a_right, None, (a,))
    (a2,) = mul(core, weight, gather_rows(v), b_right, (1.0, coef_linear), (v,), limit=MOST)

    a2_right = gather_plane(a2)
    (h,) = mul(core, weight, gather_rows(a2), b_right, (1.0, coef_linear), (a2,))
    weights = (coef_quintic, coef_cubic, coef_linear)
    wide, rest = mul(core, weight, gather_rows(h), a2_right, weights, (h, b), halves=True, limit=MOST)
    wide, rest, order = lax.optimization_barrier((wide, rest, order))
    panel = call(panel_kernel, [struct(16, SUB, COLS)], (1, 8), "panel", 0)(order, *early, *late)[0]
    panel = panel.reshape(ALL, COLS)

    parts = gather_parts(wide, rest)
    head = trade_roles(apply(0, HALF, weight, pos, upper, lower, panel, parts[:2] + parts[4:6]))
    tail = trade_roles(apply(HALF, REST, weight, pos, upper, lower, panel, parts[2:4] + parts[6:]))
    return jnp.concatenate([head, tail], 0).astype(F32)


def solution(mesh):
    split = Mesh(mesh.devices.reshape(SIZES), NAMES)
    placed = P(("z", "xh"), ("xl", "y", "c"))
    return jax.shard_map(body, mesh=split, in_specs=(placed,), out_specs=placed, check_vma=False)
```

```python
import functools
import math

import jax
import jax.numpy as jnp
import numpy as np
from jax import lax
from jax.experimental import pallas as pl
from jax.experimental.pallas import tpu as pltpu
from jax.sharding import Mesh, PartitionSpec as P

coef_linear = 3.4445
coef_cubic = -4.775
coef_quintic = 2.0315

NAMES = ("z", "xh", "xl", "y", "c")
SIZES = (4, 2, 2, 4, 2)
PLANE = ("xh", "xl", "y")
BF = jnp.bfloat16
F32 = jnp.float32
ROWS = 448
SUB = 224
TAIL = 240
COLS = 1152
ALL = 3584
TILE = 128
WIDE = 512
VMEM = 20 * 1024 * 1024
MOST = 57 * 1024 * 1024
HALF = 256
REST = ROWS - HALF

def flat(pos):
    index = 0
    for value, size in zip(pos, SIZES):
        index = index * size + value
    return index


def move(value, target):
    every = [(z, a, b, y, c) for z in range(4) for a in range(2) for b in range(2) for y in range(4) for c in range(2)]
    return lax.ppermute(value, NAMES, [(flat(pos), flat(target(*pos))) for pos in every])


def swap_z(value, by):
    return move(value, lambda z, xh, xl, y, c: (z ^ by, xh, xl, y, c))


def along_x(value, step):
    def target(z, xh, xl, y, c):
        x = (xh * 2 + xl - step) % 4
        return (z, x // 2, x % 2, y, c)

    return move(value, target)


def along_y(value, step):
    return move(value, lambda z, xh, xl, y, c: (z, xh, xl, (y - step) % 4, c))


def swap_x(value, by):
    return move(value, lambda z, xh, xl, y, c: (z, xh ^ (by >> 1), xl ^ (by & 1), y, c))


def swap_y(value, by):
    return move(value, lambda z, xh, xl, y, c: (z, xh, xl, y ^ by, c))


def other_core(value):
    return move(value, lambda z, xh, xl, y, c: (z, xh, xl, y, 1 - c))


def trade_roles(value):
    return move(value, lambda z, xh, xl, y, c: (z, c, xl, y, xh))


def struct(*shape, dtype=BF):
    return jax.ShapeDtypeStruct(shape, dtype)


def call(kernel, shapes, counts, name, flops, scratch=(), scalars_out=0, limit=VMEM):
    smem, vmem = counts
    n = len(shapes)
    return pl.pallas_call(
        kernel,
        out_shape=shapes,
        in_specs=[pl.BlockSpec(memory_space=pltpu.SMEM)] * smem + [pl.BlockSpec(memory_space=pltpu.VMEM)] * vmem,
        out_specs=[pl.BlockSpec(memory_space=pltpu.VMEM)] * (n - scalars_out)
        + [pl.BlockSpec(memory_space=pltpu.SMEM)] * scalars_out,
        scratch_shapes=list(scratch),
        compiler_params=pltpu.CompilerParams(vmem_limit_bytes=limit),
        cost_estimate=pl.CostEstimate(flops=flops, bytes_accessed=6 << 20, transcendentals=0),
        name=name,
    )


def split_value(value):
    lane = lax.broadcasted_iota(jnp.int32, (16, TILE), 1)
    whole = jnp.full((16, TILE), value, F32)
    high = whole.astype(BF).astype(F32)
    middle = (whole - high).astype(BF).astype(F32)
    low = whole - high - middle
    out = jnp.where(lane == 0, high, jnp.where(lane == 1, middle, jnp.where(lane == 2, low, 0.0)))
    return out.astype(BF)


def cast_kernel(in_ref, upper_ref, lower_ref):
    squares = jnp.zeros((8, COLS), F32)
    for i in range(0, ROWS, 32):
        block = in_ref[i : i + 32, :]
        if i < SUB:
            upper_ref[i : i + 32, :] = block.astype(BF)
        else:
            lower_ref[i - SUB : i - SUB + 32, :] = block.astype(BF)
        square = block * block
        squares += (square[:8] + square[8:16]) + (square[16:24] + square[24:])
    lower_ref[SUB:, :] = jnp.zeros((TAIL - SUB, COLS), BF)
    lower_ref[SUB:, :TILE] = split_value(jnp.sum(squares))


def cast(momentum):
    return call(cast_kernel, [struct(SUB, COLS), struct(TAIL, COLS)], (0, 1), "cast", 0)(momentum)


def pieces(refs):
    for ref in refs:
        step = ref.shape[0] // 2
        for i in range(2):
            yield ref[i * step : i * step + SUB, :]


def sum_of_squares(refs):
    total = jnp.zeros((16, TILE), F32)
    for ref in refs:
        if ref.shape[0] == 2 * TAIL:
            for i in range(2):
                total += ref[i * TAIL + SUB : (i + 1) * TAIL, :TILE].astype(F32)
    return jnp.sum(total) * 0.0625


def turn(upper_ref, lower_ref, turned):
    turned[:, :SUB] = upper_ref[:SUB, :].T
    turned[:, SUB:] = lower_ref[:SUB, :].T


def first_gram_kernel(upper_ref, lower_ref, out_ref, turned):
    turn(upper_ref, lower_ref, turned)
    gram_kernel(turned, upper_ref, lower_ref, out_ref)


def gram_kernel(turned_ref, *refs):
    for i, piece in enumerate(pieces(refs[:-1])):
        refs[-1][i] = jnp.dot(piece, turned_ref[...], preferred_element_type=F32).astype(BF)


def first_gram(upper, lower):
    flops = 2 * 4 * SUB * ROWS * COLS
    shapes = [struct(4, SUB, ROWS), struct(COLS, ROWS)]
    return call(first_gram_kernel, shapes, (0, 2), "gram", flops)(upper, lower)


def gram(turned, *parts):
    flops = 2 * 4 * SUB * ROWS * COLS
    return call(gram_kernel, [struct(4, SUB, ROWS)], (0, 1 + len(parts)), "gram", flops)(turned, *parts)[0]


def gram_more_kernel(count, index_ref, turned, done_ref, more_ref, *refs):
    parts, fresh, outs = refs[:count], refs[count : 2 * count], refs[2 * count : 2 * count + 8]
    value_ref, full = refs[2 * count + 8], refs[2 * count + 9 :]

    def store(n, block):
        for q in range(4):
            end = min(TILE, ROWS - q * TILE)
            full[q][index_ref[q * 16 + n], :, :end] = block[:, q * TILE : q * TILE + end]

    for n in range(4):
        store(n, done_ref[n])
        store(4 + n, more_ref[n])
    for n, piece in enumerate(pieces(fresh)):
        store(2 * count + n, jnp.dot(piece, turned[...], preferred_element_type=F32).astype(BF))
    for q in range(4):
        end = min(TILE, ROWS - q * TILE)
        for half in range(2):
            outs[2 * q + half][:, :, :end] = full[q][half * 8 : half * 8 + 8, :, :end]
            if end < TILE:
                outs[2 * q + half][:, :, end:] = jnp.zeros((8, SUB, TILE - end), BF)
    value_ref[0] = sum_of_squares(refs[: 2 * count])


def gram_more(index, turned, done, more, parts, fresh):
    count = len(parts)
    return call(
        functools.partial(gram_more_kernel, count),
        [struct(8, SUB, TILE)] * 8 + [struct(1, dtype=F32)],
        (1, 3 + 2 * count),
        "gram",
        2 * 2 * count * SUB * ROWS * COLS,
        [pltpu.VMEM((16, SUB, TILE), BF)] * 4,
        scalars_out=1,
    )(index, turned, done, more, *parts, *fresh)


def panel_kernel(order_ref, *refs):
    parts, out_ref = refs[:-1], refs[-1]
    for i, piece in enumerate(pieces(parts)):
        out_ref[order_ref[i]] = piece


def halve_kernel(*refs):
    keep, got, outs = refs[:4], refs[4:8], refs[8:]
    for q in range(4):
        for i in range(8):
            total = keep[q][i].astype(F32) + got[q][i].astype(F32)
            outs[2 * q + i // 4][i % 4] = total.astype(BF)


def unstack_kernel(*refs):
    keep, got, outs = refs[:4], refs[4:8], refs[8:]
    for q in range(4):
        at = (q % 2) * TILE
        for i in range(4):
            total = keep[q][i].astype(F32) + got[q][i].astype(F32)
            outs[(q // 2) * 4 + i][:, at : at + TILE] = total.astype(BF)


def sum_kernel(value_ref, *refs):
    wides, rests, (out_ref, wide_ref, rest_ref) = refs[:4], refs[4:8], refs[8:]
    for refs, sum_ref in ((wides, wide_ref), (rests, rest_ref)):
        total = refs[0][...].astype(F32)
        for ref in refs[1:]:
            total += ref[...].astype(F32)
        sum_ref[...] = total.astype(BF)
    rest_ref[:16, REST:] = split_value(value_ref[0])[:, : HALF - REST]
    out_ref[:, :HALF] = wide_ref[...]
    out_ref[:, HALF:] = rest_ref[...]


def scatter_plane(split, value):
    keep, send = split[0::2], split[1::2]
    got = [swap_y(send[0], 3), swap_y(send[1], 1), swap_x(send[2], 3), swap_x(send[3], 1)]
    split = call(halve_kernel, [struct(4, SUB, TILE)] * 8, (0, 8), "halve", 0)(*keep, *got)
    keep, send = split[0::2], split[1::2]
    got = [swap_y(send[0], 1), swap_y(send[1], 3), swap_x(send[2], 1), swap_x(send[3], 3)]
    halves = call(unstack_kernel, [struct(SUB, HALF)] * 8, (0, 8), "unstack", 0)(*keep, *got)
    wides = [halves[0]] + [along_x(halves[s], -s) for s in (1, 2, 3)]
    rests = [halves[4]] + [along_y(halves[4 + s], -s) for s in (1, 2, 3)]
    shapes = [struct(SUB, WIDE), struct(SUB, HALF), struct(SUB, HALF)]
    return call(sum_kernel, shapes, (1, 8), "sum", 0)(value, *wides, *rests)


def stack_kernel(*refs):
    for n, outs in ((0, refs[8:10]), (4, refs[10:12])):
        for i in range(4):
            outs[0][i] = refs[n + i][:, :TILE]
            outs[1][i] = refs[n + i][:, TILE:]


def join_kernel(*refs):
    mine, got, outs = refs[:4], refs[4:8], refs[8:]
    for q in range(4):
        outs[q][:4] = mine[q][...]
        outs[q][4:] = got[q][...]


def gather_parts(wide, rest):
    wides = [wide] + [along_x(wide, s) for s in (1, 2, 3)]
    rests = [rest] + [along_y(rest, s) for s in (1, 2, 3)]
    parts = call(stack_kernel, [struct(4, SUB, TILE)] * 4, (0, 8), "stack", 0)(*wides, *rests)
    got = [swap_y(parts[0], 1), swap_y(parts[1], 3), swap_x(parts[2], 1), swap_x(parts[3], 3)]
    parts = call(join_kernel, [struct(8, SUB, TILE)] * 4, (0, 8), "join", 0)(*parts, *got)
    got = [swap_y(parts[0], 3), swap_y(parts[1], 1), swap_x(parts[2], 3), swap_x(parts[3], 1)]
    return [*parts, *got]


def place(pos_ref, refs, right, first=0):
    x, y = pos_ref[0], pos_ref[1]
    for q in range(first, first + len(refs) // 2):
        at = (q - first) * TILE
        end = min(TILE, right.shape[1] - at)
        near, far = ((1, 3), (3, 1))[q % 2]
        for i in range(16):
            by = (0, near, far, near ^ far)[i // 4]
            if q < 2:
                share = lax.rem(x + i % 4, 4) * 4 + (y ^ by)
            else:
                share = (x ^ by) * 4 + lax.rem(y + i % 4, 4)
            rows = pl.ds(pl.multiple_of(share * SUB, SUB), SUB)
            right[rows, at : at + end] = refs[q - first + (i // 8) * (len(refs) // 2)][i % 8, :, :end]


def product(core_ref, mine_ref, other_ref, right, left):
    first = core_ref[0] == 0
    for i in range(4):
        mine, other = mine_ref[i, :, :ROWS], other_ref[i, :, :ROWS]
        left[:, i * 896 : i * 896 + ROWS] = jnp.where(first, mine, other)
        left[:, i * 896 + ROWS : (i + 1) * 896] = jnp.where(first, other, mine)
    return jnp.dot(left[...], right[:, :ROWS], preferred_element_type=F32)


def first_kernel(core_ref, pos_ref, *refs):
    lefts, (share_ref, right_ref, out_ref, weight_ref, left) = refs[:4], refs[4:]
    squares = jnp.zeros((16, WIDE - ROWS), F32)
    for i in range(16):
        squares += right_ref[i * SUB : i * SUB + 16, ROWS:].astype(F32)
    squares = jnp.sum(squares) * 0.0625
    scale = 1.0 / (jnp.sqrt(jnp.full((8, TILE), squares, F32)) + 1e-07)
    scale = jnp.max(scale)
    twice = scale * scale
    first = core_ref[0] == 0
    for i, by in enumerate((0, 1, 3, 2)):
        rows = slice(i % 2 * SUB, (i % 2 + 1) * SUB)
        mine, other = lefts[i // 2][rows, :ROWS], lefts[2 + i // 2][rows, :ROWS]
        line = jnp.concatenate([jnp.where(first, mine, other), jnp.where(first, other, mine)], 1)
        left[:, pl.ds(pl.multiple_of((pos_ref[2] ^ by) * 896, TILE), 896)] = line
    total = jnp.dot(left[...], right_ref[:, :ROWS], preferred_element_type=F32)
    total = total * twice * (coef_quintic * twice) + (coef_cubic * twice) * share_ref[:, :ROWS].astype(F32)
    out_ref[...] = total.astype(BF)
    weight_ref[0] = twice
    weight_ref[1] = coef_linear * twice
    weight_ref[2] = scale * math.sqrt(18432)


def place_kernel(pos_ref, *refs):
    place(pos_ref, refs[:8], refs[8])


def first_mul(core, pos, lefts, share, right):
    return call(
        first_kernel,
        [struct(SUB, ROWS), struct(3, dtype=F32)],
        (2, 6),
        "first_mul",
        2 * SUB * ROWS * ALL,
        [pltpu.VMEM((SUB, ALL), BF)],
        scalars_out=1,
    )(core, pos, *lefts, share, right)


def mul_kernel(weights, count, core_ref, weight_ref, mine_ref, other_ref, right_ref, *refs):
    extras, outs, left = refs[:count], refs[count:-1], refs[-1]
    if weights is None:
        weights = [weight_ref[0], weight_ref[1]]
    total = product(core_ref, mine_ref, other_ref, right_ref, left) * weights[0]
    for weight, extra in zip(weights[1:], extras):
        total += weight * extra[:, :ROWS].astype(F32)
    total = total.astype(BF)
    if len(outs) == 1:
        outs[0][...] = total
    else:
        outs[0][...] = total[:, :HALF]
        outs[1][:, :REST] = total[:, HALF:]
        outs[1][:, REST:] = jnp.zeros((SUB, HALF - REST), BF)


def mul(core, weight, lefts, right, weights, extras, halves=False, limit=VMEM):
    return call(
        functools.partial(mul_kernel, weights, len(extras)),
        [struct(SUB, HALF)] * 2 if halves else [struct(SUB, ROWS)],
        (2, 3 + len(extras)),
        "mul",
        2 * SUB * ROWS * ALL,
        [pltpu.VMEM((SUB, ALL), BF)],
        limit=limit,
    )(core, weight, *lefts, right, *extras)


def own_rows(upper_ref, lower_ref, first, end):
    for base, ref in ((0, upper_ref), (SUB, lower_ref)):
        low, high = max(first, base), min(end, base + SUB)
        if low < high:
            yield low - first, ref[low - base : high - base, :]


def apply_kernel(first, weight_ref, pos_ref, upper_ref, lower_ref, panel_ref, *refs):
    parts, (out_ref, right, mat) = refs[:4], refs[4:]
    rows = out_ref.shape[0]
    place(pos_ref, parts, right, first // TILE)
    for k in range(4):
        mat[:, k * 896 : (k + 1) * 896] = right[k * 896 : (k + 1) * 896, :].T
    total = jnp.dot(mat[...], panel_ref[...], preferred_element_type=F32)
    linear = coef_linear * coef_linear
    for at, own in own_rows(upper_ref, lower_ref, first, first + rows):
        some = slice(at, at + own.shape[0])
        result = (total[some, :] + linear * own.astype(F32)) * weight_ref[2]
        out_ref[some, :] = result.astype(BF)


def apply(first, rows, weight, pos, upper, lower, panel, parts):
    return call(
        functools.partial(apply_kernel, first),
        [struct(rows, COLS)],
        (2, 7),
        "apply",
        2 * ALL * rows * COLS,
        [pltpu.VMEM((ALL, rows), BF), pltpu.VMEM((rows, ALL), BF)],
    )(weight, pos, upper, lower, panel, *parts)[0]


def gather_rows(value):
    mine = lax.all_gather(value, "z")
    return [mine, other_core(mine)]


def gather_plane(value):
    return lax.all_gather(value, PLANE, axis=0, tiled=True)


def body(momentum):
    z, c = (lax.axis_index(name).astype(jnp.int32) for name in ("z", "c"))
    core = c.reshape(1)
    x = (lax.axis_index("xh") * 2 + lax.axis_index("xl")).astype(jnp.int32)
    y = lax.axis_index("y").astype(jnp.int32)
    pos = jnp.stack([x, y, z])

    upper, lower = (trade_roles(value) for value in cast(momentum))
    upper_1 = swap_z(upper, 1)
    lower_3 = swap_z(lower, 3)
    uppers = jnp.concatenate([upper, upper_1], 0)
    lowers = jnp.concatenate([lower, lower_3], 0)
    uppers_3 = swap_z(uppers, 3)
    lowers_1 = swap_z(lowers, 1)
    done, turned = first_gram(uppers, lowers)
    near_0, near_1, uppers_3, lowers_1, done = lax.optimization_barrier((uppers, lowers, uppers_3, lowers_1, done))
    early = [uppers, lowers, uppers_3, lowers_1]
    late = [other_core(part) for part in (uppers_3, lowers_1, near_0, near_1)]
    more = gram(turned, uppers_3, lowers_1)
    near_at, far_at = ((0, 0), (1, 0), (0, 1), (3, 1)), ((3, 0), (2, 0), (1, 1), (2, 1))
    places = [(by, 0, half) for by, half in near_at + far_at] + [(by, 1, half) for by, half in far_at + near_at]
    by, swap, half = (np.array(column, np.int32) for column in zip(*places))
    piece_x = z ^ by
    piece_y = (c ^ swap) * 2 + half
    order = piece_x * 4 + piece_y

    gray_x, gray_y = ((e ^ (e >> 1)) * 4 for e in (piece_x ^ x, piece_y ^ y))
    flip_x, flip_y = (((g & 4) * 2 + (g >> 1 & 4)) for g in (gray_x, gray_y))
    far_x, far_y = (piece_x - x) & 3, (piece_y - y) & 3
    index = jnp.concatenate([gray_y + far_x, flip_y + far_x, gray_x + far_y, flip_x + far_y])
    *split, value = gram_more(index, turned, done, more, early, late)
    a, wide, rest = scatter_plane(split, value)
    near = jnp.concatenate([a, swap_z(a, 1)], 0)
    far = swap_z(near, 3)
    lefts = [near, far, other_core(near), other_core(far)]
    a_right = call(place_kernel, [struct(ALL, WIDE)], (1, 8), "place", 0)(pos, *gather_parts(wide, rest))[0]
    b, weight = first_mul(core, pos, lefts, a, a_right)

    b_right = gather_plane(b)
    (v,) = mul(core, weight, gather_rows(b), a_right, None, (a,))
    (a2,) = mul(core, weight, gather_rows(v), b_right, (1.0, coef_linear), (v,), limit=MOST)

    a2_right = gather_plane(a2)
    (h,) = mul(core, weight, gather_rows(a2), b_right, (1.0, coef_linear), (a2,))
    weights = (coef_quintic, coef_cubic, coef_linear)
    wide, rest = mul(core, weight, gather_rows(h), a2_right, weights, (h, b), halves=True, limit=MOST)
    wide, rest, order = lax.optimization_barrier((wide, rest, order))
    panel = call(panel_kernel, [struct(16, SUB, COLS)], (1, 8), "panel", 0)(order, *early, *late)[0]
    panel = panel.reshape(ALL, COLS)

    parts = gather_parts(wide, rest)
    head = trade_roles(apply(0, HALF, weight, pos, upper, lower, panel, parts[:2] + parts[4:6]))
    tail = trade_roles(apply(HALF, REST, weight, pos, upper, lower, panel, parts[2:4] + parts[6:]))
    return jnp.concatenate([head, tail], 0).astype(F32)


def solution(mesh):
    split = Mesh(mesh.devices.reshape(SIZES), NAMES)
    placed = P(("z", "xh"), ("xl", "y", "c"))
    return jax.shard_map(body, mesh=split, in_specs=(placed,), out_specs=placed, check_vma=False)
```

```python
import functools
import math

import jax
import jax.numpy as jnp
import numpy as np
from jax import lax
from jax.experimental import pallas as pl
from jax.experimental.pallas import tpu as pltpu
from jax.sharding import Mesh, PartitionSpec as P

coef_linear = 3.4445
coef_cubic = -4.775
coef_quintic = 2.0315

NAMES = ("z", "xh", "xl", "y", "c")
SIZES = (4, 2, 2, 4, 2)
PLANE = ("xh", "xl", "y")
BF = jnp.bfloat16
F32 = jnp.float32
ROWS = 448
SUB = 224
TAIL = 240
COLS = 1152
ALL = 3584
TILE = 128
WIDE = 512
VMEM = 20 * 1024 * 1024
MOST = 57 * 1024 * 1024
HALF = 256
REST = ROWS - HALF

def flat(pos):
    index = 0
    for value, size in zip(pos, SIZES):
        index = index * size + value
    return index


def move(value, target):
    every = [(z, a, b, y, c) for z in range(4) for a in range(2) for b in range(2) for y in range(4) for c in range(2)]
    return lax.ppermute(value, NAMES, [(flat(pos), flat(target(*pos))) for pos in every])


def swap_z(value, by):
    return move(value, lambda z, xh, xl, y, c: (z ^ by, xh, xl, y, c))


def along_x(value, step):
    def target(z, xh, xl, y, c):
        x = (xh * 2 + xl - step) % 4
        return (z, x // 2, x % 2, y, c)

    return move(value, target)


def along_y(value, step):
    return move(value, lambda z, xh, xl, y, c: (z, xh, xl, (y - step) % 4, c))


def swap_x(value, by):
    return move(value, lambda z, xh, xl, y, c: (z, xh ^ (by >> 1), xl ^ (by & 1), y, c))


def swap_y(value, by):
    return move(value, lambda z, xh, xl, y, c: (z, xh, xl, y ^ by, c))


def other_core(value):
    return move(value, lambda z, xh, xl, y, c: (z, xh, xl, y, 1 - c))


def trade_roles(value):
    return move(value, lambda z, xh, xl, y, c: (z, c, xl, y, xh))


def struct(*shape, dtype=BF):
    return jax.ShapeDtypeStruct(shape, dtype)


def call(kernel, shapes, counts, name, flops, scratch=(), scalars_out=0, limit=VMEM):
    smem, vmem = counts
    n = len(shapes)
    return pl.pallas_call(
        kernel,
        out_shape=shapes,
        in_specs=[pl.BlockSpec(memory_space=pltpu.SMEM)] * smem + [pl.BlockSpec(memory_space=pltpu.VMEM)] * vmem,
        out_specs=[pl.BlockSpec(memory_space=pltpu.VMEM)] * (n - scalars_out)
        + [pl.BlockSpec(memory_space=pltpu.SMEM)] * scalars_out,
        scratch_shapes=list(scratch),
        compiler_params=pltpu.CompilerParams(vmem_limit_bytes=limit),
        cost_estimate=pl.CostEstimate(flops=flops, bytes_accessed=6 << 20, transcendentals=0),
        name=name,
    )


def split_value(value):
    lane = lax.broadcasted_iota(jnp.int32, (16, TILE), 1)
    whole = jnp.full((16, TILE), value, F32)
    high = whole.astype(BF).astype(F32)
    middle = (whole - high).astype(BF).astype(F32)
    low = whole - high - middle
    out = jnp.where(lane == 0, high, jnp.where(lane == 1, middle, jnp.where(lane == 2, low, 0.0)))
    return out.astype(BF)


def cast_kernel(in_ref, upper_ref, lower_ref):
    squares = jnp.zeros((8, COLS), F32)
    for i in range(0, ROWS, 32):
        block = in_ref[i : i + 32, :]
        if i < SUB:
            upper_ref[i : i + 32, :] = block.astype(BF)
        else:
            lower_ref[i - SUB : i - SUB + 32, :] = block.astype(BF)
        square = block * block
        squares += (square[:8] + square[8:16]) + (square[16:24] + square[24:])
    lower_ref[SUB:, :] = jnp.zeros((TAIL - SUB, COLS), BF)
    lower_ref[SUB:, :TILE] = split_value(jnp.sum(squares))


def cast(momentum):
    return call(cast_kernel, [struct(SUB, COLS), struct(TAIL, COLS)], (0, 1), "cast", 0)(momentum)


def pieces(refs):
    for ref in refs:
        step = ref.shape[0] // 2
        for i in range(2):
            yield ref[i * step : i * step + SUB, :]


def sum_of_squares(refs):
    total = jnp.zeros((16, TILE), F32)
    for ref in refs:
        if ref.shape[0] == 2 * TAIL:
            for i in range(2):
                total += ref[i * TAIL + SUB : (i + 1) * TAIL, :TILE].astype(F32)
    return jnp.sum(total) * 0.0625


def turn(upper_ref, lower_ref, turned):
    turned[:, :SUB] = upper_ref[:SUB, :].T
    turned[:, SUB:] = lower_ref[:SUB, :].T


def first_gram_kernel(upper_ref, lower_ref, out_ref, turned):
    turn(upper_ref, lower_ref, turned)
    gram_kernel(turned, upper_ref, lower_ref, out_ref)


def gram_kernel(turned_ref, *refs):
    for i, piece in enumerate(pieces(refs[:-1])):
        refs[-1][i] = jnp.dot(piece, turned_ref[...], preferred_element_type=F32).astype(BF)


def first_gram(upper, lower):
    flops = 2 * 4 * SUB * ROWS * COLS
    shapes = [struct(4, SUB, ROWS), struct(COLS, ROWS)]
    return call(first_gram_kernel, shapes, (0, 2), "gram", flops)(upper, lower)


def gram(turned, *parts):
    flops = 2 * 4 * SUB * ROWS * COLS
    return call(gram_kernel, [struct(4, SUB, ROWS)], (0, 1 + len(parts)), "gram", flops)(turned, *parts)[0]


def gram_more_kernel(count, index_ref, turned, done_ref, more_ref, *refs):
    parts, fresh, outs = refs[:count], refs[count : 2 * count], refs[2 * count : 2 * count + 8]
    value_ref, full = refs[2 * count + 8], refs[2 * count + 9 :]

    def store(n, block):
        for q in range(4):
            end = min(TILE, ROWS - q * TILE)
            full[q][index_ref[q * 16 + n], :, :end] = block[:, q * TILE : q * TILE + end]

    for n in range(4):
        store(n, done_ref[n])
        store(4 + n, more_ref[n])
    for n, piece in enumerate(pieces(fresh)):
        store(2 * count + n, jnp.dot(piece, turned[...], preferred_element_type=F32).astype(BF))
    for q in range(4):
        end = min(TILE, ROWS - q * TILE)
        for half in range(2):
            outs[2 * q + half][:, :, :end] = full[q][half * 8 : half * 8 + 8, :, :end]
            if end < TILE:
                outs[2 * q + half][:, :, end:] = jnp.zeros((8, SUB, TILE - end), BF)
    value_ref[0] = sum_of_squares(refs[: 2 * count])


def gram_more(index, turned, done, more, parts, fresh):
    count = len(parts)
    return call(
        functools.partial(gram_more_kernel, count),
        [struct(8, SUB, TILE)] * 8 + [struct(1, dtype=F32)],
        (1, 3 + 2 * count),
        "gram",
        2 * 2 * count * SUB * ROWS * COLS,
        [pltpu.VMEM((16, SUB, TILE), BF)] * 4,
        scalars_out=1,
    )(index, turned, done, more, *parts, *fresh)


def panel_kernel(order_ref, *refs):
    parts, out_ref = refs[:-1], refs[-1]
    for i, piece in enumerate(pieces(parts)):
        out_ref[order_ref[i]] = piece


def halve_kernel(*refs):
    keep, got, outs = refs[:4], refs[4:8], refs[8:]
    for q in range(4):
        for i in range(8):
            total = keep[q][i].astype(F32) + got[q][i].astype(F32)
            outs[2 * q + i // 4][i % 4] = total.astype(BF)


def unstack_kernel(*refs):
    keep, got, outs = refs[:4], refs[4:8], refs[8:]
    for q in range(4):
        at = (q % 2) * TILE
        for i in range(4):
            total = keep[q][i].astype(F32) + got[q][i].astype(F32)
            outs[(q // 2) * 4 + i][:, at : at + TILE] = total.astype(BF)


def sum_kernel(value_ref, *refs):
    wides, rests, (out_ref, wide_ref, rest_ref) = refs[:4], refs[4:8], refs[8:]
    for refs, sum_ref in ((wides, wide_ref), (rests, rest_ref)):
        total = refs[0][...].astype(F32)
        for ref in refs[1:]:
            total += ref[...].astype(F32)
        sum_ref[...] = total.astype(BF)
    rest_ref[:16, REST:] = split_value(value_ref[0])[:, : HALF - REST]
    out_ref[:, :HALF] = wide_ref[...]
    out_ref[:, HALF:] = rest_ref[...]


def scatter_plane(split, value):
    keep, send = split[0::2], split[1::2]
    got = [swap_y(send[0], 3), swap_y(send[1], 1), swap_x(send[2], 3), swap_x(send[3], 1)]
    split = call(halve_kernel, [struct(4, SUB, TILE)] * 8, (0, 8), "halve", 0)(*keep, *got)
    keep, send = split[0::2], split[1::2]
    got = [swap_y(send[0], 1), swap_y(send[1], 3), swap_x(send[2], 1), swap_x(send[3], 3)]
    halves = call(unstack_kernel, [struct(SUB, HALF)] * 8, (0, 8), "unstack", 0)(*keep, *got)
    wides = [halves[0]] + [along_x(halves[s], -s) for s in (1, 2, 3)]
    rests = [halves[4]] + [along_y(halves[4 + s], -s) for s in (1, 2, 3)]
    shapes = [struct(SUB, WIDE), struct(SUB, HALF), struct(SUB, HALF)]
    return call(sum_kernel, shapes, (1, 8), "sum", 0)(value, *wides, *rests)


def stack_kernel(*refs):
    for n, outs in ((0, refs[8:10]), (4, refs[10:12])):
        for i in range(4):
            outs[0][i] = refs[n + i][:, :TILE]
            outs[1][i] = refs[n + i][:, TILE:]


def join_kernel(*refs):
    mine, got, outs = refs[:4], refs[4:8], refs[8:]
    for q in range(4):
        outs[q][:4] = mine[q][...]
        outs[q][4:] = got[q][...]


def gather_parts(wide, rest):
    wides = [wide] + [along_x(wide, s) for s in (1, 2, 3)]
    rests = [rest] + [along_y(rest, s) for s in (1, 2, 3)]
    parts = call(stack_kernel, [struct(4, SUB, TILE)] * 4, (0, 8), "stack", 0)(*wides, *rests)
    got = [swap_y(parts[0], 1), swap_y(parts[1], 3), swap_x(parts[2], 1), swap_x(parts[3], 3)]
    parts = call(join_kernel, [struct(8, SUB, TILE)] * 4, (0, 8), "join", 0)(*parts, *got)
    got = [swap_y(parts[0], 3), swap_y(parts[1], 1), swap_x(parts[2], 3), swap_x(parts[3], 1)]
    return [*parts, *got]


def place(pos_ref, refs, right, first=0):
    x, y = pos_ref[0], pos_ref[1]
    for q in range(first, first + len(refs) // 2):
        at = (q - first) * TILE
        end = min(TILE, right.shape[1] - at)
        near, far = ((1, 3), (3, 1))[q % 2]
        for i in range(16):
            by = (0, near, far, near ^ far)[i // 4]
            if q < 2:
                share = lax.rem(x + i % 4, 4) * 4 + (y ^ by)
            else:
                share = (x ^ by) * 4 + lax.rem(y + i % 4, 4)
            rows = pl.ds(pl.multiple_of(share * SUB, SUB), SUB)
            right[rows, at : at + end] = refs[q - first + (i // 8) * (len(refs) // 2)][i % 8, :, :end]


def product(core_ref, mine_ref, other_ref, right, left):
    first = core_ref[0] == 0
    for i in range(4):
        mine, other = mine_ref[i, :, :ROWS], other_ref[i, :, :ROWS]
        left[:, i * 896 : i * 896 + ROWS] = jnp.where(first, mine, other)
        left[:, i * 896 + ROWS : (i + 1) * 896] = jnp.where(first, other, mine)
    return jnp.dot(left[...], right[:, :ROWS], preferred_element_type=F32)


def first_kernel(core_ref, pos_ref, *refs):
    lefts, (share_ref, right_ref, out_ref, weight_ref, left) = refs[:4], refs[4:]
    squares = jnp.zeros((16, WIDE - ROWS), F32)
    for i in range(16):
        squares += right_ref[i * SUB : i * SUB + 16, ROWS:].astype(F32)
    squares = jnp.sum(squares) * 0.0625
    scale = 1.0 / (jnp.sqrt(jnp.full((8, TILE), squares, F32)) + 1e-07)
    scale = jnp.max(scale)
    twice = scale * scale
    first = core_ref[0] == 0
    for i, by in enumerate((0, 1, 3, 2)):
        rows = slice(i % 2 * SUB, (i % 2 + 1) * SUB)
        mine, other = lefts[i // 2][rows, :ROWS], lefts[2 + i // 2][rows, :ROWS]
        line = jnp.concatenate([jnp.where(first, mine, other), jnp.where(first, other, mine)], 1)
        left[:, pl.ds(pl.multiple_of((pos_ref[2] ^ by) * 896, TILE), 896)] = line
    total = jnp.dot(left[...], right_ref[:, :ROWS], preferred_element_type=F32)
    total = total * twice * (coef_quintic * twice) + (coef_cubic * twice) * share_ref[:, :ROWS].astype(F32)
    out_ref[...] = total.astype(BF)
    weight_ref[0] = twice
    weight_ref[1] = coef_linear * twice
    weight_ref[2] = scale * math.sqrt(18432)


def place_kernel(pos_ref, *refs):
    place(pos_ref, refs[:8], refs[8])


def first_mul(core, pos, lefts, share, right):
    return call(
        first_kernel,
        [struct(SUB, ROWS), struct(3, dtype=F32)],
        (2, 6),
        "first_mul",
        2 * SUB * ROWS * ALL,
        [pltpu.VMEM((SUB, ALL), BF)],
        scalars_out=1,
    )(core, pos, *lefts, share, right)


def mul_kernel(weights, count, core_ref, weight_ref, mine_ref, other_ref, right_ref, *refs):
    extras, outs, left = refs[:count], refs[count:-1], refs[-1]
    if weights is None:
        weights = [weight_ref[0], weight_ref[1]]
    total = product(core_ref, mine_ref, other_ref, right_ref, left) * weights[0]
    for weight, extra in zip(weights[1:], extras):
        total += weight * extra[:, :ROWS].astype(F32)
    total = total.astype(BF)
    if len(outs) == 1:
        outs[0][...] = total
    else:
        outs[0][...] = total[:, :HALF]
        outs[1][:, :REST] = total[:, HALF:]
        outs[1][:, REST:] = jnp.zeros((SUB, HALF - REST), BF)


def mul(core, weight, lefts, right, weights, extras, halves=False, limit=VMEM):
    return call(
        functools.partial(mul_kernel, weights, len(extras)),
        [struct(SUB, HALF)] * 2 if halves else [struct(SUB, ROWS)],
        (2, 3 + len(extras)),
        "mul",
        2 * SUB * ROWS * ALL,
        [pltpu.VMEM((SUB, ALL), BF)],
        limit=limit,
    )(core, weight, *lefts, right, *extras)


def own_rows(upper_ref, lower_ref, first, end):
    for base, ref in ((0, upper_ref), (SUB, lower_ref)):
        low, high = max(first, base), min(end, base + SUB)
        if low < high:
            yield low - first, ref[low - base : high - base, :]


def apply_kernel(first, weight_ref, pos_ref, upper_ref, lower_ref, panel_ref, *refs):
    parts, (out_ref, right, mat) = refs[:4], refs[4:]
    rows = out_ref.shape[0]
    place(pos_ref, parts, right, first // TILE)
    for k in range(4):
        mat[:, k * 896 : (k + 1) * 896] = right[k * 896 : (k + 1) * 896, :].T
    total = jnp.dot(mat[...], panel_ref[...], preferred_element_type=F32)
    linear = coef_linear * coef_linear
    for at, own in own_rows(upper_ref, lower_ref, first, first + rows):
        some = slice(at, at + own.shape[0])
        result = (total[some, :] + linear * own.astype(F32)) * weight_ref[2]
        out_ref[some, :] = result.astype(BF)


def apply(first, rows, weight, pos, upper, lower, panel, parts):
    return call(
        functools.partial(apply_kernel, first),
        [struct(rows, COLS)],
        (2, 7),
        "apply",
        2 * ALL * rows * COLS,
        [pltpu.VMEM((ALL, rows), BF), pltpu.VMEM((rows, ALL), BF)],
    )(weight, pos, upper, lower, panel, *parts)[0]


def gather_rows(value):
    mine = lax.all_gather(value, "z")
    return [mine, other_core(mine)]


def gather_plane(value):
    return lax.all_gather(value, PLANE, axis=0, tiled=True)


def body(momentum):
    z, c = (lax.axis_index(name).astype(jnp.int32) for name in ("z", "c"))
    core = c.reshape(1)
    x = (lax.axis_index("xh") * 2 + lax.axis_index("xl")).astype(jnp.int32)
    y = lax.axis_index("y").astype(jnp.int32)
    pos = jnp.stack([x, y, z])

    upper, lower = (trade_roles(value) for value in cast(momentum))
    upper_1 = swap_z(upper, 1)
    lower_3 = swap_z(lower, 3)
    uppers = jnp.concatenate([upper, upper_1], 0)
    lowers = jnp.concatenate([lower, lower_3], 0)
    uppers_3 = swap_z(uppers, 3)
    lowers_1 = swap_z(lowers, 1)
    done, turned = first_gram(uppers, lowers)
    near_0, near_1, lowers_1, done = lax.optimization_barrier((uppers, lowers, lowers_1, done))
    early = [uppers, lowers, uppers_3, lowers_1]
    late = [other_core(part) for part in (uppers_3, lowers_1, near_0, near_1)]
    more = gram(turned, uppers_3, lowers_1)
    near_at, far_at = ((0, 0), (1, 0), (0, 1), (3, 1)), ((3, 0), (2, 0), (1, 1), (2, 1))
    places = [(by, 0, half) for by, half in near_at + far_at] + [(by, 1, half) for by, half in far_at + near_at]
    by, swap, half = (np.array(column, np.int32) for column in zip(*places))
    piece_x = z ^ by
    piece_y = (c ^ swap) * 2 + half
    order = piece_x * 4 + piece_y

    gray_x, gray_y = ((e ^ (e >> 1)) * 4 for e in (piece_x ^ x, piece_y ^ y))
    flip_x, flip_y = (((g & 4) * 2 + (g >> 1 & 4)) for g in (gray_x, gray_y))
    far_x, far_y = (piece_x - x) & 3, (piece_y - y) & 3
    index = jnp.concatenate([gray_y + far_x, flip_y + far_x, gray_x + far_y, flip_x + far_y])
    *split, value = gram_more(index, turned, done, more, early, late)
    a, wide, rest = scatter_plane(split, value)
    near = jnp.concatenate([a, swap_z(a, 1)], 0)
    far = swap_z(near, 3)
    lefts = [near, far, other_core(near), other_core(far)]
    a_right = call(place_kernel, [struct(ALL, WIDE)], (1, 8), "place", 0)(pos, *gather_parts(wide, rest))[0]
    b, weight = first_mul(core, pos, lefts, a, a_right)

    b_right = gather_plane(b)
    (v,) = mul(core, weight, gather_rows(b), a_right, None, (a,))
    (a2,) = mul(core, weight, gather_rows(v), b_right, (1.0, coef_linear), (v,), limit=MOST)

    a2_right = gather_plane(a2)
    (h,) = mul(core, weight, gather_rows(a2), b_right, (1.0, coef_linear), (a2,))
    weights = (coef_quintic, coef_cubic, coef_linear)
    wide, rest = mul(core, weight, gather_rows(h), a2_right, weights, (h, b), halves=True, limit=MOST)
    wide, rest, order = lax.optimization_barrier((wide, rest, order))
    panel = call(panel_kernel, [struct(16, SUB, COLS)], (1, 8), "panel", 0)(order, *early, *late)[0]
    panel = panel.reshape(ALL, COLS)

    parts = gather_parts(wide, rest)
    head = trade_roles(apply(0, HALF, weight, pos, upper, lower, panel, parts[:2] + parts[4:6]))
    tail = trade_roles(apply(HALF, REST, weight, pos, upper, lower, panel, parts[2:4] + parts[6:]))
    return jnp.concatenate([head, tail], 0).astype(F32)


def solution(mesh):
    split = Mesh(mesh.devices.reshape(SIZES), NAMES)
    placed = P(("z", "xh"), ("xl", "y", "c"))
    return jax.shard_map(body, mesh=split, in_specs=(placed,), out_specs=placed, check_vma=False)
```

```python
import functools
import math

import jax
import jax.numpy as jnp
import numpy as np
from jax import lax
from jax.experimental import pallas as pl
from jax.experimental.pallas import tpu as pltpu
from jax.sharding import Mesh, PartitionSpec as P

coef_linear = 3.4445
coef_cubic = -4.775
coef_quintic = 2.0315

NAMES = ("z", "xh", "xl", "y", "c")
SIZES = (4, 2, 2, 4, 2)
PLANE = ("xh", "xl", "y")
BF = jnp.bfloat16
F32 = jnp.float32
ROWS = 448
SUB = 224
TAIL = 240
COLS = 1152
ALL = 3584
TILE = 128
WIDE = 512
VMEM = 20 * 1024 * 1024
MOST = 57 * 1024 * 1024
HALF = 256
REST = ROWS - HALF

def flat(pos):
    index = 0
    for value, size in zip(pos, SIZES):
        index = index * size + value
    return index


def move(value, target):
    every = [(z, a, b, y, c) for z in range(4) for a in range(2) for b in range(2) for y in range(4) for c in range(2)]
    return lax.ppermute(value, NAMES, [(flat(pos), flat(target(*pos))) for pos in every])


def swap_z(value, by):
    return move(value, lambda z, xh, xl, y, c: (z ^ by, xh, xl, y, c))


def along_x(value, step):
    def target(z, xh, xl, y, c):
        x = (xh * 2 + xl - step) % 4
        return (z, x // 2, x % 2, y, c)

    return move(value, target)


def along_y(value, step):
    return move(value, lambda z, xh, xl, y, c: (z, xh, xl, (y - step) % 4, c))


def swap_x(value, by):
    return move(value, lambda z, xh, xl, y, c: (z, xh ^ (by >> 1), xl ^ (by & 1), y, c))


def swap_y(value, by):
    return move(value, lambda z, xh, xl, y, c: (z, xh, xl, y ^ by, c))


def other_core(value):
    return move(value, lambda z, xh, xl, y, c: (z, xh, xl, y, 1 - c))


def trade_roles(value):
    return move(value, lambda z, xh, xl, y, c: (z, c, xl, y, xh))


def struct(*shape, dtype=BF):
    return jax.ShapeDtypeStruct(shape, dtype)


def call(kernel, shapes, counts, name, flops, scratch=(), scalars_out=0, limit=VMEM):
    smem, vmem = counts
    n = len(shapes)
    return pl.pallas_call(
        kernel,
        out_shape=shapes,
        in_specs=[pl.BlockSpec(memory_space=pltpu.SMEM)] * smem + [pl.BlockSpec(memory_space=pltpu.VMEM)] * vmem,
        out_specs=[pl.BlockSpec(memory_space=pltpu.VMEM)] * (n - scalars_out)
        + [pl.BlockSpec(memory_space=pltpu.SMEM)] * scalars_out,
        scratch_shapes=list(scratch),
        compiler_params=pltpu.CompilerParams(vmem_limit_bytes=limit),
        cost_estimate=pl.CostEstimate(flops=flops, bytes_accessed=6 << 20, transcendentals=0),
        name=name,
    )


def split_value(value):
    lane = lax.broadcasted_iota(jnp.int32, (16, TILE), 1)
    whole = jnp.full((16, TILE), value, F32)
    high = whole.astype(BF).astype(F32)
    middle = (whole - high).astype(BF).astype(F32)
    low = whole - high - middle
    out = jnp.where(lane == 0, high, jnp.where(lane == 1, middle, jnp.where(lane == 2, low, 0.0)))
    return out.astype(BF)


def cast_kernel(in_ref, upper_ref, lower_ref):
    squares = jnp.zeros((8, COLS), F32)
    for i in range(0, ROWS, 32):
        block = in_ref[i : i + 32, :]
        if i < SUB:
            upper_ref[i : i + 32, :] = block.astype(BF)
        else:
            lower_ref[i - SUB : i - SUB + 32, :] = block.astype(BF)
        square = block * block
        squares += (square[:8] + square[8:16]) + (square[16:24] + square[24:])
    lower_ref[SUB:, :] = jnp.zeros((TAIL - SUB, COLS), BF)
    lower_ref[SUB:, :TILE] = split_value(jnp.sum(squares))


def cast(momentum):
    return call(cast_kernel, [struct(SUB, COLS), struct(TAIL, COLS)], (0, 1), "cast", 0)(momentum)


def pieces(refs):
    for ref in refs:
        step = ref.shape[0] // 2
        for i in range(2):
            yield ref[i * step : i * step + SUB, :]


def sum_of_squares(refs):
    total = jnp.zeros((16, TILE), F32)
    for ref in refs:
        if ref.shape[0] == 2 * TAIL:
            for i in range(2):
                total += ref[i * TAIL + SUB : (i + 1) * TAIL, :TILE].astype(F32)
    return jnp.sum(total) * 0.0625


def turn(upper_ref, lower_ref, turned):
    turned[:, :SUB] = upper_ref[:SUB, :].T
    turned[:, SUB:] = lower_ref[:SUB, :].T


def first_gram_kernel(upper_ref, lower_ref, out_ref, turned):
    turn(upper_ref, lower_ref, turned)
    gram_kernel(turned, upper_ref, lower_ref, out_ref)


def gram_kernel(turned_ref, *refs):
    for i, piece in enumerate(pieces(refs[:-1])):
        refs[-1][i] = jnp.dot(piece, turned_ref[...], preferred_element_type=F32).astype(BF)


def first_gram(upper, lower):
    flops = 2 * 4 * SUB * ROWS * COLS
    shapes = [struct(4, SUB, ROWS), struct(COLS, ROWS)]
    return call(first_gram_kernel, shapes, (0, 2), "gram", flops)(upper, lower)


def gram(turned, *parts):
    flops = 2 * 4 * SUB * ROWS * COLS
    return call(gram_kernel, [struct(4, SUB, ROWS)], (0, 1 + len(parts)), "gram", flops)(turned, *parts)[0]


def gram_more_kernel(count, index_ref, turned, done_ref, more_ref, *refs):
    parts, fresh, outs = refs[:count], refs[count : 2 * count], refs[2 * count : 2 * count + 8]
    value_ref, full = refs[2 * count + 8], refs[2 * count + 9 :]

    def store(n, block):
        for q in range(4):
            end = min(TILE, ROWS - q * TILE)
            full[q][index_ref[q * 16 + n], :, :end] = block[:, q * TILE : q * TILE + end]

    for n in range(4):
        store(n, done_ref[n])
        store(4 + n, more_ref[n])
    for n, piece in enumerate(pieces(fresh)):
        store(2 * count + n, jnp.dot(piece, turned[...], preferred_element_type=F32).astype(BF))
    for q in range(4):
        end = min(TILE, ROWS - q * TILE)
        for half in range(2):
            outs[2 * q + half][:, :, :end] = full[q][half * 8 : half * 8 + 8, :, :end]
            if end < TILE:
                outs[2 * q + half][:, :, end:] = jnp.zeros((8, SUB, TILE - end), BF)
    value_ref[0] = sum_of_squares(refs[: 2 * count])


def gram_more(index, turned, done, more, parts, fresh):
    count = len(parts)
    return call(
        functools.partial(gram_more_kernel, count),
        [struct(8, SUB, TILE)] * 8 + [struct(1, dtype=F32)],
        (1, 3 + 2 * count),
        "gram",
        2 * 2 * count * SUB * ROWS * COLS,
        [pltpu.VMEM((16, SUB, TILE), BF)] * 4,
        scalars_out=1,
    )(index, turned, done, more, *parts, *fresh)


def panel_kernel(order_ref, *refs):
    parts, out_ref = refs[:-1], refs[-1]
    for i, piece in enumerate(pieces(parts)):
        out_ref[order_ref[i]] = piece


def halve_kernel(*refs):
    keep, got, outs = refs[:4], refs[4:8], refs[8:]
    for q in range(4):
        for i in range(8):
            total = keep[q][i].astype(F32) + got[q][i].astype(F32)
            outs[2 * q + i // 4][i % 4] = total.astype(BF)


def unstack_kernel(*refs):
    keep, got, outs = refs[:4], refs[4:8], refs[8:]
    for q in range(4):
        at = (q % 2) * TILE
        for i in range(4):
            total = keep[q][i].astype(F32) + got[q][i].astype(F32)
            outs[(q // 2) * 4 + i][:, at : at + TILE] = total.astype(BF)


def sum_kernel(value_ref, *refs):
    wides, rests, (out_ref, wide_ref, rest_ref) = refs[:4], refs[4:8], refs[8:]
    for refs, sum_ref in ((wides, wide_ref), (rests, rest_ref)):
        total = refs[0][...].astype(F32)
        for ref in refs[1:]:
            total += ref[...].astype(F32)
        sum_ref[...] = total.astype(BF)
    rest_ref[:16, REST:] = split_value(value_ref[0])[:, : HALF - REST]
    out_ref[:, :HALF] = wide_ref[...]
    out_ref[:, HALF:] = rest_ref[...]


def scatter_plane(split, value):
    keep, send = split[0::2], split[1::2]
    got = [swap_y(send[0], 3), swap_y(send[1], 1), swap_x(send[2], 3), swap_x(send[3], 1)]
    split = call(halve_kernel, [struct(4, SUB, TILE)] * 8, (0, 8), "halve", 0)(*keep, *got)
    keep, send = split[0::2], split[1::2]
    got = [swap_y(send[0], 1), swap_y(send[1], 3), swap_x(send[2], 1), swap_x(send[3], 3)]
    halves = call(unstack_kernel, [struct(SUB, HALF)] * 8, (0, 8), "unstack", 0)(*keep, *got)
    wides = [halves[0]] + [along_x(halves[s], -s) for s in (1, 2, 3)]
    rests = [halves[4]] + [along_y(halves[4 + s], -s) for s in (1, 2, 3)]
    shapes = [struct(SUB, WIDE), struct(SUB, HALF), struct(SUB, HALF)]
    return call(sum_kernel, shapes, (1, 8), "sum", 0)(value, *wides, *rests)


def stack_kernel(*refs):
    for n, outs in ((0, refs[8:10]), (4, refs[10:12])):
        for i in range(4):
            outs[0][i] = refs[n + i][:, :TILE]
            outs[1][i] = refs[n + i][:, TILE:]


def join_kernel(*refs):
    mine, got, outs = refs[:4], refs[4:8], refs[8:]
    for q in range(4):
        outs[q][:4] = mine[q][...]
        outs[q][4:] = got[q][...]


def gather_parts(wide, rest):
    wides = [wide] + [along_x(wide, s) for s in (1, 2, 3)]
    rests = [rest] + [along_y(rest, s) for s in (1, 2, 3)]
    parts = call(stack_kernel, [struct(4, SUB, TILE)] * 4, (0, 8), "stack", 0)(*wides, *rests)
    got = [swap_y(parts[0], 1), swap_y(parts[1], 3), swap_x(parts[2], 1), swap_x(parts[3], 3)]
    parts = call(join_kernel, [struct(8, SUB, TILE)] * 4, (0, 8), "join", 0)(*parts, *got)
    got = [swap_y(parts[0], 3), swap_y(parts[1], 1), swap_x(parts[2], 3), swap_x(parts[3], 1)]
    return [*parts, *got]


def place(pos_ref, refs, right, first=0):
    x, y = pos_ref[0], pos_ref[1]
    for q in range(first, first + len(refs) // 2):
        at = (q - first) * TILE
        end = min(TILE, right.shape[1] - at)
        near, far = ((1, 3), (3, 1))[q % 2]
        for i in range(16):
            by = (0, near, far, near ^ far)[i // 4]
            if q < 2:
                share = lax.rem(x + i % 4, 4) * 4 + (y ^ by)
            else:
                share = (x ^ by) * 4 + lax.rem(y + i % 4, 4)
            rows = pl.ds(pl.multiple_of(share * SUB, SUB), SUB)
            right[rows, at : at + end] = refs[q - first + (i // 8) * (len(refs) // 2)][i % 8, :, :end]


def product(core_ref, mine_ref, other_ref, right, left):
    first = core_ref[0] == 0
    for i in range(4):
        mine, other = mine_ref[i, :, :ROWS], other_ref[i, :, :ROWS]
        left[:, i * 896 : i * 896 + ROWS] = jnp.where(first, mine, other)
        left[:, i * 896 + ROWS : (i + 1) * 896] = jnp.where(first, other, mine)
    return jnp.dot(left[...], right[:, :ROWS], preferred_element_type=F32)


def first_kernel(core_ref, pos_ref, *refs):
    lefts, (share_ref, right_ref, out_ref, weight_ref, left) = refs[:4], refs[4:]
    squares = jnp.zeros((16, WIDE - ROWS), F32)
    for i in range(16):
        squares += right_ref[i * SUB : i * SUB + 16, ROWS:].astype(F32)
    squares = jnp.sum(squares) * 0.0625
    scale = 1.0 / (jnp.sqrt(jnp.full((8, TILE), squares, F32)) + 1e-07)
    scale = jnp.max(scale)
    twice = scale * scale
    first = core_ref[0] == 0
    for i, by in enumerate((0, 1, 3, 2)):
        rows = slice(i % 2 * SUB, (i % 2 + 1) * SUB)
        mine, other = lefts[i // 2][rows, :ROWS], lefts[2 + i // 2][rows, :ROWS]
        line = jnp.concatenate([jnp.where(first, mine, other), jnp.where(first, other, mine)], 1)
        left[:, pl.ds(pl.multiple_of((pos_ref[2] ^ by) * 896, TILE), 896)] = line
    total = jnp.dot(left[...], right_ref[:, :ROWS], preferred_element_type=F32)
    total = total * twice * (coef_quintic * twice) + (coef_cubic * twice) * share_ref[:, :ROWS].astype(F32)
    out_ref[...] = total.astype(BF)
    weight_ref[0] = twice
    weight_ref[1] = coef_linear * twice
    weight_ref[2] = scale * math.sqrt(18432)


def place_kernel(pos_ref, *refs):
    place(pos_ref, refs[:8], refs[8])


def first_mul(core, pos, lefts, share, right):
    return call(
        first_kernel,
        [struct(SUB, ROWS), struct(3, dtype=F32)],
        (2, 6),
        "first_mul",
        2 * SUB * ROWS * ALL,
        [pltpu.VMEM((SUB, ALL), BF)],
        scalars_out=1,
    )(core, pos, *lefts, share, right)


def mul_kernel(weights, count, core_ref, weight_ref, mine_ref, other_ref, right_ref, *refs):
    extras, outs, left = refs[:count], refs[count:-1], refs[-1]
    if weights is None:
        weights = [weight_ref[0], weight_ref[1]]
    total = product(core_ref, mine_ref, other_ref, right_ref, left) * weights[0]
    for weight, extra in zip(weights[1:], extras):
        total += weight * extra[:, :ROWS].astype(F32)
    total = total.astype(BF)
    if len(outs) == 1:
        outs[0][...] = total
    else:
        outs[0][...] = total[:, :HALF]
        outs[1][:, :REST] = total[:, HALF:]
        outs[1][:, REST:] = jnp.zeros((SUB, HALF - REST), BF)


def mul(core, weight, lefts, right, weights, extras, halves=False, limit=VMEM):
    return call(
        functools.partial(mul_kernel, weights, len(extras)),
        [struct(SUB, HALF)] * 2 if halves else [struct(SUB, ROWS)],
        (2, 3 + len(extras)),
        "mul",
        2 * SUB * ROWS * ALL,
        [pltpu.VMEM((SUB, ALL), BF)],
        limit=limit,
    )(core, weight, *lefts, right, *extras)


def own_rows(upper_ref, lower_ref, first, end):
    for base, ref in ((0, upper_ref), (SUB, lower_ref)):
        low, high = max(first, base), min(end, base + SUB)
        if low < high:
            yield low - first, ref[low - base : high - base, :]


def apply_kernel(first, weight_ref, pos_ref, upper_ref, lower_ref, panel_ref, *refs):
    parts, (out_ref, right, mat) = refs[:4], refs[4:]
    rows = out_ref.shape[0]
    place(pos_ref, parts, right, first // TILE)
    for k in range(4):
        mat[:, k * 896 : (k + 1) * 896] = right[k * 896 : (k + 1) * 896, :].T
    total = jnp.dot(mat[...], panel_ref[...], preferred_element_type=F32)
    linear = coef_linear * coef_linear
    for at, own in own_rows(upper_ref, lower_ref, first, first + rows):
        some = slice(at, at + own.shape[0])
        result = (total[some, :] + linear * own.astype(F32)) * weight_ref[2]
        out_ref[some, :] = result.astype(BF)


def apply(first, rows, weight, pos, upper, lower, panel, parts):
    return call(
        functools.partial(apply_kernel, first),
        [struct(rows, COLS)],
        (2, 7),
        "apply",
        2 * ALL * rows * COLS,
        [pltpu.VMEM((ALL, rows), BF), pltpu.VMEM((rows, ALL), BF)],
    )(weight, pos, upper, lower, panel, *parts)[0]


def gather_rows(value):
    mine = lax.all_gather(value, "z")
    return [mine, other_core(mine)]


def gather_plane(value):
    return lax.all_gather(value, PLANE, axis=0, tiled=True)


def body(momentum):
    z, c = (lax.axis_index(name).astype(jnp.int32) for name in ("z", "c"))
    core = c.reshape(1)
    x = (lax.axis_index("xh") * 2 + lax.axis_index("xl")).astype(jnp.int32)
    y = lax.axis_index("y").astype(jnp.int32)
    pos = jnp.stack([x, y, z])

    upper, lower = (trade_roles(value) for value in cast(momentum))
    upper_1 = swap_z(upper, 1)
    lower_3 = swap_z(lower, 3)
    uppers = jnp.concatenate([upper, upper_1], 0)
    lowers = jnp.concatenate([lower, lower_3], 0)
    uppers_3 = swap_z(uppers, 3)
    lowers_1 = swap_z(lowers, 1)
    done, turned = first_gram(uppers, lowers)
    near_0, near_1, lowers_1, done = lax.optimization_barrier((uppers, lowers, lowers_1, done))
    early = [uppers, lowers, uppers_3, lowers_1]
    late = [other_core(part) for part in (uppers_3, lowers_1, near_0, near_1)]
    more = gram(turned, uppers_3, lowers_1)
    near_at, far_at = ((0, 0), (1, 0), (0, 1), (3, 1)), ((3, 0), (2, 0), (1, 1), (2, 1))
    places = [(by, 0, half) for by, half in near_at + far_at] + [(by, 1, half) for by, half in far_at + near_at]
    by, swap, half = (np.array(column, np.int32) for column in zip(*places))
    piece_x = z ^ by
    piece_y = (c ^ swap) * 2 + half
    order = piece_x * 4 + piece_y

    gray_x, gray_y = ((e ^ (e >> 1)) * 4 for e in (piece_x ^ x, piece_y ^ y))
    flip_x, flip_y = (((g & 4) * 2 + (g >> 1 & 4)) for g in (gray_x, gray_y))
    far_x, far_y = (piece_x - x) & 3, (piece_y - y) & 3
    index = jnp.concatenate([gray_y + far_x, flip_y + far_x, gray_x + far_y, flip_x + far_y])
    *split, value = gram_more(index, turned, done, more, early, late)
    a, wide, rest = scatter_plane(split, value)
    near = jnp.concatenate([a, swap_z(a, 1)], 0)
    far = swap_z(near, 3)
    lefts = [near, far, other_core(near), other_core(far)]
    a_right = call(place_kernel, [struct(ALL, WIDE)], (1, 8), "place", 0)(pos, *gather_parts(wide, rest))[0]
    b, weight = first_mul(core, pos, lefts, a, a_right)

    b_right = gather_plane(b)
    (v,) = mul(core, weight, gather_rows(b), a_right, None, (a,))
    (a2,) = mul(core, weight, gather_rows(v), b_right, (1.0, coef_linear), (v,), limit=MOST)

    a2_right = gather_plane(a2)
    (h,) = mul(core, weight, gather_rows(a2), b_right, (1.0, coef_linear), (a2,))
    weights = (coef_quintic, coef_cubic, coef_linear)
    wide, rest = mul(core, weight, gather_rows(h), a2_right, weights, (h, b), halves=True, limit=MOST)
    wide, rest, order = lax.optimization_barrier((wide, rest, order))
    panel = call(panel_kernel, [struct(16, SUB, COLS)], (1, 8), "panel", 0)(order, *early, *late)[0]
    panel = panel.reshape(ALL, COLS)

    parts = gather_parts(wide, rest)
    tail = trade_roles(apply(HALF, REST, weight, pos, upper, lower, panel, parts[2:4] + parts[6:]))
    head = trade_roles(apply(0, HALF, weight, pos, upper, lower, panel, parts[:2] + parts[4:6]))
    return jnp.concatenate([head, tail], 0).astype(F32)


def solution(mesh):
    split = Mesh(mesh.devices.reshape(SIZES), NAMES)
    placed = P(("z", "xh"), ("xl", "y", "c"))
    return jax.shard_map(body, mesh=split, in_specs=(placed,), out_specs=placed, check_vma=False)
```
